32 devices in a mesh: rows: 4 (over y, x), frames: 8 (over z, core).
Axes of the slice: x: 2, y: 2, z: 4, core: 2. Of those that a mesh axis runs over, the one named last changes fastest.
Arguments:
- images: bfloat16 [3072, 64, 192], P('frames', 'rows'), may hold values from -6 to 6
- enc_kernel: bfloat16 [4, 4, 3, 48], replicated, may hold values from -0.875 to 0.875
- emb_weight: bfloat16 [1536, 512], P('rows'), may hold values from -0.15625 to 0.15625
- ln1_gain: float32 [512], replicated, may hold values from 0.1 to 1.9
- qkv_weight: bfloat16 [512, 1536], replicated, may hold values from -0.25 to 0.25
- out_weight: bfloat16 [512, 512], replicated, may hold values from -0.5 to 0.5
- ln2_gain: float32 [512], replicated, may hold values from 0.1 to 1.9
- up_weight: bfloat16 [512, 2048], replicated, may hold values from -0.25 to 0.25
- down_weight: bfloat16 [2048, 512], replicated, may hold values from -0.125 to 0.125
- prior_weight: bfloat16 [512, 1024], replicated, may hold values from -0.25 to 0.25
- film_scale: bfloat16 [512, 48], replicated, may hold values from -0.125 to 0.125
- film_shift: bfloat16 [512, 1536], P(None, 'rows'), may hold values from -0.25 to 0.25
- dec_kernel: bfloat16 [4, 4, 48, 3], replicated, may hold values from -0.4375 to 0.4375
- horizons: int32 [192], P('frames'), may hold values from 5 to 15
- frame_valid: int32 [3072], P('frames'), may hold values 0 or 1
- recon_cot: bfloat16 [3072, 64, 192], P('frames', 'rows'), may hold values from -6 to 6
- logit_cot: bfloat16 [3072, 1024], P('frames'), may hold values from -6 to 6
Outputs:
- rebuilt_images: bfloat16 [3072, 64, 192], P('frames', 'rows')
- image_grad: float32 [3072, 64, 192], P('frames', 'rows')
- enc_kernel_grad: float32 [4, 4, 3, 48], replicated
- emb_weight_grad: float32 [1536, 512], P('rows')
- ln1_gain_grad: float32 [512], replicated
- qkv_weight_grad: float32 [512, 1536], replicated
- out_weight_grad: float32 [512, 512], replicated
- ln2_gain_grad: float32 [512], replicated
- up_weight_grad: float32 [512, 2048], replicated
- down_weight_grad: float32 [2048, 512], replicated
- prior_weight_grad: float32 [512, 1024], replicated
- film_scale_grad: float32 [512, 48], replicated
- film_shift_grad: float32 [512, 1536], P(None, 'rows')
- dec_kernel_grad: float32 [4, 4, 48, 3], replicated
The draws below stay inside these ranges and needn't reach their ends.
All inputs are finite; a program needn't handle non-finite values. No bound on the sum of `frame_valid` on one device may be relied on, other than what follows from the above.
Results may differ from the reference program's by a relative error of at most 0.035.
Values may be sent and summed in bfloat16 or wider, within the bound.
No kernel may reach another device: no remote copies, remote signals or barrier semaphores. Data moves between devices by JAX's collectives and lax.ppermute only.
A program may use at most 384 MiB of HBM per device.

```python
import math
import jax
import jax.numpy as jnp
from jax import lax

D = 512
HEADS = 8
HD = 64
FF = 2048
CLS = 32
IMG = 64
CIN = 3
CH = 48
SLOTS = 16
ROLLOUTS = 192
TOKENS = 3072
MAP = 32


def touch_ends(result, own_key, least, largest):
    shape = result.shape
    index_at = [jax.random.randint(jax.random.fold_in(own_key, axis), (), 0, shape[axis]) for axis in range(len(shape))]
    result = result.at[tuple(index_at)].set(least)
    longest = shape.index(max(shape))
    index_at[longest] = (index_at[longest] + 1) % shape[longest]
    return result.at[tuple(index_at)].set(largest)


def shard_levels(own_key, dims, split, low, high):
    level, own = 1.0, jax.random.fold_in(own_key, 6)
    for position, shards_of in split:
        draws = jnp.exp(jax.random.uniform(jax.random.fold_in(own, position), (shards_of,), jnp.float32, low / len(split), high / len(split)))
        level = level * jnp.repeat(draws, dims[position] // shards_of).reshape([-1 if axis == position else 1 for axis in range(len(dims))])
    return level


def gaussian(stream_key, dims, width, most, split=(), kind=jnp.bfloat16):
    array = width * jax.random.normal(stream_key, dims, jnp.float32)
    if split:
        array = array * shard_levels(stream_key, dims, split, -0.22, 0.18)
    return jnp.clip(array, -most, most).astype(kind)


def setup_inputs(seed: int = 0) -> dict:
    seeds = jax.random.split(jax.random.key(seed), 18)
    return {
        "images": gaussian(seeds[0], (TOKENS, IMG, IMG * CIN), 1.0, 6.0, ((0, 8), (1, 4))),
        "enc_kernel": gaussian(seeds[1], (4, 4, CIN, CH), (16 * CIN) ** -0.5, 0.875),
        "emb_weight": gaussian(seeds[2], (MAP * CH, D), (MAP * CH) ** -0.5, 0.15625, ((0, 4),)),
        "ln1_gain": jnp.clip(1.0 + 0.18 * jax.random.normal(seeds[3], (D,), jnp.float32), 0.1, 1.9),
        "qkv_weight": gaussian(seeds[4], (D, 3 * D), D ** -0.5, 0.25),
        "out_weight": gaussian(seeds[5], (D, D), (D // 4) ** -0.5, 0.5),
        "ln2_gain": jnp.clip(1.0 + 0.18 * jax.random.normal(seeds[6], (D,), jnp.float32), 0.1, 1.9),
        "up_weight": gaussian(seeds[7], (D, FF), D ** -0.5, 0.25),
        "down_weight": gaussian(seeds[8], (FF, D), FF ** -0.5, 0.125),
        "prior_weight": gaussian(seeds[9], (D, CLS * CLS), D ** -0.5, 0.25),
        "film_scale": gaussian(seeds[10], (D, CH), (4 * D) ** -0.5, 0.125),
        "film_shift": gaussian(seeds[11], (D, MAP * CH), D ** -0.5, 0.25, ((1, 4),)),
        "dec_kernel": gaussian(seeds[12], (4, 4, CH, CIN), (4 * CH) ** -0.5, 0.4375),
        "horizons": touch_ends(jax.random.randint(seeds[13], (ROLLOUTS,), 5, SLOTS), jax.random.fold_in(seeds[13], 1), 5, SLOTS - 1).astype(jnp.int32),
        "frame_valid": touch_ends((jax.random.randint(seeds[14], (TOKENS,), 0, 4) < 3).astype(jnp.int32), jax.random.fold_in(seeds[14], 1), 0, 1),
        "recon_cot": gaussian(seeds[15], (TOKENS, IMG, IMG * CIN), 1.0, 6.0, ((0, 8), (1, 4))),
        "logit_cot": gaussian(seeds[16], (TOKENS, CLS * CLS), 1.0, 6.0, ((0, 8),)),
    }


@jax.custom_vjp
def low(v):
    return lax.optimization_barrier(v.astype(jnp.bfloat16)).astype(jnp.float32)

@jax.custom_vjp
def low_back(v):
    return v

def low_keep(v):
    return (low(v), None)

def low_pass(kept, grad):
    return (grad,)

def back_keep(v):
    return (v, None)

def back_low(kept, grad):
    return (low(grad),)
low.defvjp(low_keep, low_pass)
low_back.defvjp(back_keep, back_low)

def gelu_tanh(value):
    return jax.nn.gelu(value, approximate=True)

def layer_norm(values, gain):
    center = values - lax.optimization_barrier(jnp.mean(values, axis=-1, keepdims=True))
    spread = lax.optimization_barrier(jnp.mean(center * center, axis=-1, keepdims=True))
    return center * lax.rsqrt(spread + 1e-05) * gain

def matmul(lhs_array, rhs_array):
    return jnp.dot(lhs_array, rhs_array, precision=lax.Precision.HIGHEST)

def attend_mask(horizon_part, slot_count):
    positions = jnp.arange(slot_count)
    causal = positions[None, :] <= positions[:, None]
    inside = positions[None, :] <= horizon_part[:, None]
    return causal[None, None, :, :] & inside[:, None, None, :]

def transformer(flat_stream, horizon_piece, ln1_gain, qkv_weight, out_weight, ln2_gain, up_weight, down_weight):
    rollouts = horizon_piece.shape[0]
    scaling = 1.0 / math.sqrt(HD)
    normed_in = low(layer_norm(flat_stream, ln1_gain))
    joined = low(low_back(matmul(normed_in, qkv_weight)))
    split_shape = (rollouts, SLOTS, HEADS, HD)
    queries = joined[:, :D].reshape(split_shape)
    keys_all = joined[:, D:2 * D].reshape(split_shape)
    values_all = joined[:, 2 * D:].reshape(split_shape)
    raw_scores = jnp.einsum('rqhd,rkhd->rhqk', queries, keys_all, precision=lax.Precision.HIGHEST) * scaling
    raw_scores = low_back(raw_scores)
    allowed = attend_mask(horizon_piece, SLOTS)
    attention = jax.nn.softmax(jnp.where(allowed, raw_scores, -1e+30), axis=-1)
    attention_low = low(attention)
    context = jnp.einsum('rhqk,rkhd->rqhd', attention_low, values_all, precision=lax.Precision.HIGHEST)
    context = low(low_back(context.reshape(rollouts * SLOTS, D)))
    middle = flat_stream + low_back(matmul(context, out_weight))
    normed_mid = low(layer_norm(middle, ln2_gain))
    raised = low_back(matmul(normed_mid, up_weight))
    activated = low(gelu_tanh(raised))
    return middle + low_back(matmul(activated, down_weight))

def forward(weights, pixels, horizon_piece, live_piece, recon_piece, logit_piece):
    enc_kernel, emb_weight, ln1_gain, qkv_weight, out_weight, ln2_gain, up_weight, down_weight, prior_weight, film_scale, film_shift, dec_kernel = weights
    frame_count = pixels.shape[0]
    spatial = pixels.reshape(frame_count, IMG, IMG, CIN)
    encoded = lax.conv_general_dilated(spatial, enc_kernel, (2, 2), ((1, 1), (1, 1)), dimension_numbers=('NHWC', 'HWIO', 'NHWC'), precision=lax.Precision.HIGHEST)
    encoded = low_back(encoded)
    features = low(gelu_tanh(encoded))
    profile = low(lax.optimization_barrier(jnp.mean(features, axis=2)))
    embedded = low_back(matmul(profile.reshape(frame_count, MAP * CH), emb_weight))
    stream_out = transformer(embedded, horizon_piece, ln1_gain, qkv_weight, out_weight, ln2_gain, up_weight, down_weight)
    state_low = low(stream_out)
    logits = low_back(matmul(state_low, prior_weight))
    scale_rows = low_back(matmul(state_low, film_scale))
    shift_rows = low_back(matmul(state_low, film_shift)).reshape(frame_count, MAP, CH)
    modulated = features * (1.0 + scale_rows[:, None, None, :]) + shift_rows[:, :, None, :]
    modulated = low_back(modulated)
    decoded = low(gelu_tanh(modulated))
    flipped = dec_kernel[::-1, ::-1]
    rebuilt = lax.conv_general_dilated(decoded, flipped, (1, 1), ((2, 2), (2, 2)), lhs_dilation=(2, 2), dimension_numbers=('NHWC', 'HWIO', 'NHWC'), precision=lax.Precision.HIGHEST)
    rebuilt = rebuilt.reshape(frame_count, IMG, IMG * CIN)
    loss_value = jnp.sum(live_piece[:, None, None] * recon_piece * rebuilt) + jnp.sum(live_piece[:, None] * logit_piece * logits)
    return (loss_value, rebuilt)

def reference(images, enc_kernel, emb_weight, ln1_gain, qkv_weight, out_weight, ln2_gain, up_weight, down_weight, prior_weight, film_scale, film_shift, dec_kernel, horizons, frame_valid, recon_cot, logit_cot):
    params = tuple((weight.astype(jnp.float32) for weight in (enc_kernel, emb_weight, ln1_gain, qkv_weight, out_weight, ln2_gain, up_weight, down_weight, prior_weight, film_scale, film_shift, dec_kernel)))
    positions = jnp.arange(TOKENS) % SLOTS
    live_mask = (positions <= jnp.repeat(horizons, SLOTS)).astype(jnp.float32) * frame_valid.astype(jnp.float32)
    block_rolls = math.gcd(ROLLOUTS, 64)
    block_count = ROLLOUTS // block_rolls
    block_frames = block_rolls * SLOTS
    pieces = (images.astype(jnp.float32).reshape(block_count, block_frames, IMG, IMG * CIN), horizons.reshape(block_count, block_rolls), live_mask.reshape(block_count, block_frames), recon_cot.astype(jnp.float32).reshape(block_count, block_frames, IMG, IMG * CIN), logit_cot.astype(jnp.float32).reshape(block_count, block_frames, CLS * CLS))

    def block_step(totals, block_piece):
        image_piece, horizon_piece, live_piece, recon_piece, logit_piece = block_piece

        def loss_of(weights, pixels):
            return forward(weights, pixels, horizon_piece, live_piece, recon_piece, logit_piece)
        loss_value, pullback, rebuilt = jax.vjp(loss_of, params, image_piece, has_aux=True)
        weight_grads, pixel_grad = pullback(jnp.ones_like(loss_value))
        totals = jax.tree.map(jnp.add, totals, weight_grads)
        return (totals, (rebuilt.astype(jnp.bfloat16), pixel_grad))
    start_totals = jax.tree.map(jnp.zeros_like, params)
    totals, outputs = lax.scan(block_step, start_totals, pieces)
    rebuilt_all = outputs[0].reshape(TOKENS, IMG, IMG * CIN)
    grad_all = outputs[1].reshape(TOKENS, IMG, IMG * CIN)
    return (rebuilt_all, grad_all, totals[0], totals[1], totals[2], totals[3], totals[4], totals[5], totals[6], totals[7], totals[8], totals[9], totals[10], totals[11])
```

```python
import functools
import math

import jax
import jax.numpy as jnp
import numpy as np
from jax import lax
from jax.experimental import pallas as pl
from jax.experimental.pallas import tpu as pltpu
from jax.sharding import PartitionSpec as P

HEADS = 8
BF = jnp.bfloat16
F32 = jnp.float32
GROUPS = 4
SLOT = 64
PAD = 8
TILE = 384
ROOT = math.sqrt(2.0 / math.pi)
CUBE = 0.044715
MIB = 1024 * 1024


def nn(lhs, rhs):
    return lax.dot_general(lhs, rhs, (((1,), (0,)), ((), ())), preferred_element_type=F32)


def nt(lhs, rhs):
    return lax.dot_general(lhs, rhs, (((1,), (1,)), ((), ())), preferred_element_type=F32)


def tn(lhs, rhs):
    return lax.dot_general(lhs, rhs, (((0,), (0,)), ((), ())), preferred_element_type=F32)


def tt(lhs, rhs):
    return lax.dot_general(lhs, rhs, (((0,), (1,)), ((), ())), preferred_element_type=F32)


SHRINK = (ROOT * CUBE) ** (1.0 / 3.0)
BEND = ROOT / SHRINK


def gelu_of_half(half):
    bend = half * ((8.0 * ROOT * CUBE) * (half * half) + 2.0 * ROOT)
    return half * (jnp.tanh(bend.astype(F32)) + 1.0).astype(BF)


def double_slope(shrunk):
    square = shrunk * shrunk
    bend = shrunk * (square + BEND)
    level = jnp.tanh(bend.astype(F32))
    rise, fall = (1.0 + level).astype(BF), (1.0 - level).astype(BF)
    return rise * (shrunk * (3.0 * square + BEND) * fall + 1.0)


def gelu_pair(value):
    square = value * value
    bend = (ROOT * CUBE) * square + ROOT
    gate = 0.5 * jnp.tanh(value * bend) + 0.5
    result = value * gate
    slope = gate + result * (1.0 - gate) * ((6.0 * ROOT * CUBE) * square + 2.0 * ROOT)
    return result, slope


def wide_sum(parts):
    total = None
    for k in range(0, len(parts), 4):
        some = parts[k : k + 4]
        while len(some) > 1:
            some = [a + b for a, b in zip(some[::2], some[1::2])]
        total = some[0].astype(F32) if total is None else total + some[0].astype(F32)
    return total


def whole(shape):
    return pl.BlockSpec(shape, lambda *_: (0,) * len(shape))


def params(mib):
    return pltpu.CompilerParams(vmem_limit_bytes=mib * MIB)


def cost(flops, nbytes, transcendentals=0):
    return pl.CostEstimate(flops=flops, bytes_accessed=nbytes, transcendentals=transcendentals)


def tap_places(taps, chan_in, copies):
    places = np.zeros((copies, taps * chan_in * taps, taps * SLOT), np.float32)
    for j in range(copies):
        for kh in range(taps):
            for c in range(chan_in):
                for kw in range(taps):
                    place = PAD - chan_in + (2 * j + kw) * chan_in + c
                    places[j, (kh * chan_in + c) * taps + kw, kh * SLOT + place] = 1.0
    return places


def expand_kernel(enc_ref, dec_ref, places_ref, enc_cols_out, enc_out, dec_cols_out, dec_out):
    for source, cols, out in ((enc_ref, enc_cols_out, enc_out), (dec_ref, dec_cols_out, dec_out)):
        taps = source[...]
        spread = jnp.concatenate([tn(taps, places_ref[j]) for j in range(places_ref.shape[0])], axis=0)
        cols[...] = spread.astype(BF)
        out[...] = jnp.transpose(spread).astype(BF)


def expand(enc_taps, dec_taps, places):
    copies, channels, size = places.shape
    width = copies * enc_taps.shape[1]
    cols = jax.ShapeDtypeStruct((width, size), BF)
    rows = jax.ShapeDtypeStruct((size, width), BF)
    return pl.pallas_call(
        expand_kernel,
        out_shape=[cols, rows, cols, rows],
        compiler_params=params(60),
        name="expand",
    )(enc_taps, dec_taps, places)


def keep_row(ring_ref, slot, row):
    ring_ref[slot, PAD : PAD + row.shape[0], :] = row


def window(ring_ref, first, taps, g, stride):
    return jnp.concatenate(
        [ring_ref[lax.rem(first + kh, 4), g * stride : g * stride + SLOT, :] for kh in range(taps)], axis=0
    )


def fold_taps(cov_ref, places_ref, channels):
    total = None
    for j in range(places_ref.shape[0]):
        term = lax.dot_general(
            places_ref[j].astype(F32),
            cov_ref[j * channels : (j + 1) * channels, :],
            (((1,), (1,)), ((), ())),
            precision=lax.Precision.HIGHEST,
            preferred_element_type=F32,
        )
        total = term if total is None else total + term
    return total


def halo_spec(halo, which):
    return pl.BlockSpec((1,) + halo.shape[1:], lambda i: (which, 0, 0))


def four_row_specs(frames, lanes, rows, base=0):
    return [
        pl.BlockSpec((1, lanes, frames), lambda i, k=k: (jnp.minimum(4 * (i + base) + k, rows - 1), 0, 0))
        for k in range(1, 5)
    ]


def fill_six(ring_scr, first, last, start, row_refs, down_ref, live=None):
    def masked(row):
        return row if live is None else (row.astype(F32) * live).astype(BF)

    @pl.when(first)
    def _():
        ring_scr[...] = jnp.zeros_like(ring_scr)
        for slot, row in enumerate(start):
            keep_row(ring_scr, slot, masked(row()))

    @pl.when(jnp.logical_not(first))
    def _():
        ring_scr[0:2] = ring_scr[4:6]

    for k, ref in enumerate(row_refs[:3]):
        keep_row(ring_scr, k + 2, masked(ref[0]))

    @pl.when(jnp.logical_not(last))
    def _():
        keep_row(ring_scr, 5, masked(row_refs[3][0]))

    @pl.when(last)
    def _():
        keep_row(ring_scr, 5, masked(down_ref[0]))


def fill_windows_at(window_scr, ring_scr, first, taps, stride):
    frames = ring_scr.shape[2]
    for g in range(GROUPS):
        for kh in range(taps):
            window_scr[kh * SLOT : (kh + 1) * SLOT, g * frames : (g + 1) * frames] = ring_scr[
                first + kh, g * stride : g * stride + SLOT, :
            ]


def add_rows(rows_scr, first, placed, g, stride):
    for kh in range(placed.shape[0] // SLOT):
        part = slice(g * stride, g * stride + SLOT)
        rows_scr[first + kh, part, :] += placed[kh * SLOT : (kh + 1) * SLOT, :]


def fill_windows(window_scr, ring_scr, first, taps, stride):
    frames = ring_scr.shape[2]
    for g in range(GROUPS):
        window_scr[:, g * frames : (g + 1) * frames] = window(ring_scr, first, taps, g, stride)


def tiles(frames, g):
    size = min(TILE, frames)
    return [(slice(t, t + size), slice(g * frames + t, g * frames + t + size)) for t in range(0, frames, size)]


def encode_row(ring_scr, first, enc_ref, feat_out, window_scr, value_scr, sum_scr, stride):
    width, depth = enc_ref.shape
    channels, frames = sum_scr.shape
    fill_windows(window_scr, ring_scr, first, depth // SLOT, stride)
    value_scr[...] = nn(enc_ref[...] * 0.5, window_scr[...])
    for g in range(GROUPS):
        for tile, column in tiles(frames, g):
            found = []
            for j in range(0, width, channels):
                low = gelu_of_half(value_scr[j : j + channels, column].astype(BF))
                feat_out[0, g * width + j : g * width + j + channels, tile] = low
                found.append(low)
            sum_scr[:, tile] = wide_sum(found) if g == 0 else sum_scr[:, tile] + wide_sum(found)
    return (sum_scr[...] * (1.0 / (GROUPS * width // channels))).astype(BF)


def encode_inner_kernel(
    odd_ref, even_ref, one_ref, two_ref, enc_ref, feat_out, profile_out, ring_scr, window_scr, value_scr, sum_scr
):
    step = pl.program_id(0)

    @pl.when(step == 0)
    def _():
        ring_scr[...] = jnp.zeros_like(ring_scr)
        keep_row(ring_scr, 2, one_ref[0])
        keep_row(ring_scr, 3, two_ref[0])

    keep_row(ring_scr, lax.rem(2 * step, 4), odd_ref[0])
    keep_row(ring_scr, lax.rem(2 * step + 1, 4), even_ref[0])
    stride = odd_ref.shape[1] // GROUPS
    profile_out[...] = encode_row(
        ring_scr, 2 * step + 2, enc_ref, feat_out, window_scr, value_scr, sum_scr, stride
    )


def encode_edge_kernel(
    a_ref, b_ref, c_ref, up_ref, down_ref, enc_ref, emb_ref, inner_ref, feat_ref,
    feat_out, profile_out, embed_out, ring_scr, window_scr, value_scr, sum_scr,
):
    del feat_ref
    step = pl.program_id(0)
    channels = sum_scr.shape[0]

    @pl.when(step == 0)
    def _():
        ring_scr[...] = jnp.zeros_like(ring_scr)
        keep_row(ring_scr, 0, up_ref[0])
        for k, ref in enumerate((a_ref, b_ref, c_ref)):
            keep_row(ring_scr, k + 1, ref[0])

    @pl.when(step == 1)
    def _():
        for k, ref in enumerate((a_ref, b_ref, c_ref)):
            keep_row(ring_scr, k, ref[0])
        keep_row(ring_scr, 3, down_ref[0])

    stride = up_ref.shape[1] // GROUPS
    profile = encode_row(ring_scr, 0, enc_ref, feat_out, window_scr, value_scr, sum_scr, stride)
    size = profile_out.shape[0]

    @pl.when(step == 0)
    def _():
        profile_out[:channels, :] = profile
        profile_out[channels : size - channels, :] = inner_ref[...]

    @pl.when(step == 1)
    def _():
        profile_out[size - channels :, :] = profile
        embed_out[...] = tn(profile_out[...], emb_ref[...]).astype(BF)


def encode_inner(image_rows, enc, channels):
    rows, lanes, frames = image_rows.shape
    map_rows = rows // 2
    width = enc.shape[0]
    line = GROUPS * width
    map_spec = pl.BlockSpec((1, line, frames), lambda i: (i + 1, 0, 0))
    map_shape = jax.ShapeDtypeStruct((map_rows, line, frames), BF)
    inner = map_rows - 2
    return pl.pallas_call(
        encode_inner_kernel,
        grid=(inner,),
        in_specs=[
            pl.BlockSpec((1, lanes, frames), lambda i: (2 * i + 3, 0, 0)),
            pl.BlockSpec((1, lanes, frames), lambda i: (2 * i + 4, 0, 0)),
            pl.BlockSpec((1, lanes, frames), lambda i: (1, 0, 0)),
            pl.BlockSpec((1, lanes, frames), lambda i: (2, 0, 0)),
            whole(enc.shape),
        ],
        out_specs=[map_spec, pl.BlockSpec((channels, frames), lambda i: (i, 0))],
        out_shape=[map_shape, jax.ShapeDtypeStruct((inner * channels, frames), BF)],
        scratch_shapes=[
            pltpu.VMEM((4, lanes + 2 * PAD, frames), BF),
            pltpu.VMEM((enc.shape[1], GROUPS * frames), BF),
            pltpu.VMEM((width, GROUPS * frames), F32),
            pltpu.VMEM((channels, frames), F32),
        ],
        compiler_params=params(60),
        cost_estimate=cost(2 * inner * frames * line * 256, 4 * inner * frames * line, inner * frames * line),
        name="encode_inner",
    )(image_rows, image_rows, image_rows, image_rows, enc)


def encode_edge(image_rows, up, down, enc, emb, inner, feat):
    rows, lanes, frames = image_rows.shape
    map_rows, line, _ = feat.shape
    width = enc.shape[0]
    channels = emb.shape[0] // map_rows
    model = emb.shape[1]
    end = map_rows - 1
    map_spec = pl.BlockSpec((1, line, frames), lambda i: (i * end, 0, 0))
    map_shape = jax.ShapeDtypeStruct(feat.shape, BF)
    profile = (map_rows * channels, frames)
    row_specs_here = [
        pl.BlockSpec((1, lanes, frames), lambda i, k=k: (i * (rows - 3) + k, 0, 0)) for k in range(3)
    ]
    return pl.pallas_call(
        encode_edge_kernel,
        grid=(2,),
        in_specs=row_specs_here
        + [halo_spec(up, 0), halo_spec(down, 0)]
        + [whole(x.shape) for x in (enc, emb, inner)]
        + [pl.BlockSpec(memory_space=pl.ANY)],
        out_specs=[map_spec, whole(profile), whole((frames, model))],
        out_shape=[
            map_shape,
            jax.ShapeDtypeStruct(profile, BF),
            jax.ShapeDtypeStruct((frames, model), BF),
        ],
        scratch_shapes=[
            pltpu.VMEM((4, lanes + 2 * PAD, frames), BF),
            pltpu.VMEM((enc.shape[1], GROUPS * frames), BF),
            pltpu.VMEM((width, GROUPS * frames), F32),
            pltpu.VMEM((channels, frames), F32),
        ],
        input_output_aliases={8: 0},
        compiler_params=params(60),
        cost_estimate=cost(4 * frames * line * 256, 8 * frames * line, 2 * frames * line),
        name="encode_edge",
    )(image_rows, image_rows, image_rows, up, down, enc, emb, inner, feat)


def normed(values):
    center = values - jnp.mean(values, axis=-1, keepdims=True)
    spread = jnp.mean(center * center, axis=-1, keepdims=True)
    inverse = lax.rsqrt(spread + 1e-05)
    return center * inverse, inverse


def stacked_heads(pair, lane):
    zero = jnp.zeros_like(pair)
    first = lane < 64
    return jnp.concatenate([jnp.where(first, pair, zero), jnp.where(first, zero, pair)], axis=0)


def fetch(sources, targets, sems):
    copies = [pltpu.make_async_copy(src, dst, sems.at[k]) for k, (src, dst) in enumerate(zip(sources, targets))]
    for copy in copies:
        copy.start()
    return copies


def send(source, target, sem):
    copy = pltpu.make_async_copy(source, target, sem)
    copy.start()
    return copy


def block_forward_kernel(
    slots, part_ref, more_ref, keys_ok_ref, ln1_ref, ln2_ref, film_scale_ref, qkv_in, out_in, up_in, down_in,
    film_shift_in, joined_out, attend_out, context_out, middle_out, active_out, slope_out, state_out, scale_out,
    shift_out, qkv_ref, out_ref, up_ref, down_ref, film_shift_ref, joined_ref, attend_ref, context_ref, middle_ref,
    active_ref, slope_ref, in_sems, out_sems,
):
    copies = fetch(
        (qkv_in, out_in, up_in, down_in, film_shift_in), (qkv_ref, out_ref, up_ref, down_ref, film_shift_ref), in_sems
    )
    embedded = part_ref[...].astype(F32) + more_ref[...].astype(F32)
    frames, model = embedded.shape
    unit, _ = normed(embedded)
    low = (unit * ln1_ref[...]).astype(BF)
    copies[0].wait()
    joined_ref[...] = nn(low, qkv_ref[...]).astype(BF)
    sent = [send(joined_ref, joined_out, out_sems.at[0])]
    size = 128
    row = lax.broadcasted_iota(jnp.int32, (size, size), 0)
    col = lax.broadcasted_iota(jnp.int32, (size, size), 1)
    inside = (row // slots == col // slots) & (col <= row)
    scaling = 1.0 / math.sqrt(model // HEADS)
    for b in range(frames // size):
        part = slice(b * size, (b + 1) * size)
        allowed = inside & (keys_ok_ref[:, part] > 0.5)
        for pair in range(HEADS // 2):
            lanes = pair * 128
            queries = joined_ref[part, lanes : lanes + 128]
            keys = stacked_heads(joined_ref[part, model + lanes : model + lanes + 128], col)
            values = stacked_heads(joined_ref[part, 2 * model + lanes : 2 * model + lanes + 128], col)
            scores = nt(queries, keys) * scaling
            halves = []
            for half in range(2):
                some = jnp.where(allowed, scores[:, half * size : (half + 1) * size], -1e30)
                weights = jnp.exp(some - jnp.max(some, axis=-1, keepdims=True))
                weights = weights / jnp.sum(weights, axis=-1, keepdims=True)
                halves.append(weights.astype(BF))
            weights = jnp.concatenate(halves, axis=1)
            attend_ref[b * HEADS // 2 + pair] = weights
            context_ref[part, lanes : lanes + 128] = nn(weights, values).astype(BF)
    sent.append(send(attend_ref, attend_out, out_sems.at[1]))
    sent.append(send(context_ref, context_out, out_sems.at[2]))
    copies[1].wait()
    middle = embedded + nn(context_ref[...], out_ref[...])
    middle_ref[...] = middle
    sent.append(send(middle_ref, middle_out, out_sems.at[3]))
    unit, _ = normed(middle)
    low = (unit * ln2_ref[...]).astype(BF)
    hidden = up_ref.shape[1]
    copies[2].wait()
    for start in range(0, hidden, 512):
        lanes = slice(start, start + 512)
        result, slope = gelu_pair(nn(low, up_ref[:, lanes]))
        active_ref[:, lanes] = result.astype(BF)
        slope_ref[:, lanes] = slope.astype(BF)
    sent.append(send(active_ref, active_out, out_sems.at[4]))
    sent.append(send(slope_ref, slope_out, out_sems.at[5]))
    copies[3].wait()
    state = (middle + nn(active_ref[...], down_ref[...])).astype(BF)
    state_out[...] = state
    scale_out[...] = nt(film_scale_ref[...], state) + 1.0
    copies[4].wait()
    shift_out[...] = tt(film_shift_ref[...], state)
    for copy in sent:
        copy.wait()


def block_forward(slots, parts, keys_ok, ln1, qkv, out_w, ln2, up_w, down_w, film_scale, film_shift):
    frames, model = parts[0].shape
    hidden = up_w.shape[1]
    blocks = frames // 128
    saved = [
        ((frames, 3 * model), BF),
        ((blocks * HEADS // 2, 128, 256), BF),
        ((frames, model), BF),
        ((frames, model), F32),
        ((frames, hidden), BF),
        ((frames, hidden), BF),
    ]
    shapes = [
        ((frames, model), BF),
        ((film_scale.shape[0], frames), F32),
        ((film_shift.shape[1], frames), F32),
    ]
    flops = 2 * frames * model * (3 * model + model + 2 * hidden)
    vmem, hbm = pl.BlockSpec(memory_space=pltpu.VMEM), pl.BlockSpec(memory_space=pl.ANY)
    staged = (qkv, out_w, up_w, down_w, film_shift)
    return pl.pallas_call(
        functools.partial(block_forward_kernel, slots),
        in_specs=[vmem] * 6 + [hbm] * len(staged),
        out_specs=[hbm] * len(saved) + [vmem] * len(shapes),
        out_shape=[jax.ShapeDtypeStruct(*s) for s in saved + shapes],
        scratch_shapes=[pltpu.VMEM(w.shape, w.dtype) for w in staged]
        + [pltpu.VMEM(*s) for s in saved]
        + [pltpu.SemaphoreType.DMA((len(staged),)), pltpu.SemaphoreType.DMA((len(saved),))],
        compiler_params=params(60),
        cost_estimate=cost(flops, 16 * 1024 * 1024, frames * hidden),
        name="block_forward",
    )(*parts, keys_ok, ln1, ln2, film_scale, *staged)


def decoded_grad_kernel(base, odd, a_ref, b_ref, c_ref, d_ref, one_ref, two_ref, down_ref, live_ref, dec_ref, *rest):
    out_ref, ring_scr, window_scr, grad_scr = rest[-4:]
    step = pl.program_id(0)
    _, lanes, frames = down_ref.shape
    width, depth = dec_ref.shape
    start = (lambda: one_ref[0], lambda: two_ref[0])
    fill_six(
        ring_scr, step == 0, step + base == odd, start, (a_ref, b_ref, c_ref, d_ref), down_ref, live_ref[...]
    )
    dec = dec_ref[...] * 0.5
    for r in range(2):
        fill_windows_at(window_scr, ring_scr, 2 * r, depth // SLOT, lanes // GROUPS)
        grad_scr[...] = nn(dec, window_scr[...])
        for g in range(GROUPS):
            for tile, column in tiles(frames, g):
                out_ref[r, g * width : (g + 1) * width, tile] = grad_scr[:, column].astype(BF)


def decoded_grad(recon_rows, up, down, live, dec_cols, base, steps, before):
    rows, lanes, frames = recon_rows.shape
    map_rows = rows // 2
    width, depth = dec_cols.shape
    line = GROUPS * width
    one = up if base == 0 else recon_rows
    row_shape = (1, lanes, frames)
    return pl.pallas_call(
        functools.partial(decoded_grad_kernel, base, map_rows // 2 - 1),
        grid=(steps,),
        in_specs=four_row_specs(frames, lanes, rows, base)
        + [
            halo_spec(up, 1) if base == 0 else pl.BlockSpec(row_shape, lambda i: (4 * base - 1, 0, 0)),
            pl.BlockSpec(row_shape, lambda i: (4 * base, 0, 0)),
            halo_spec(down, 1),
            whole(live.shape),
            whole(dec_cols.shape),
        ]
        + [pl.BlockSpec(memory_space=pl.ANY)] * len(before),
        out_specs=pl.BlockSpec((2, line, frames), lambda i: (i + base, 0, 0)),
        out_shape=jax.ShapeDtypeStruct((map_rows, line, frames), BF),
        scratch_shapes=[
            pltpu.VMEM((6, lanes + 2 * PAD, frames), BF),
            pltpu.VMEM((depth, GROUPS * frames), BF),
            pltpu.VMEM((width, GROUPS * frames), F32),
        ],
        input_output_aliases={9: 0} if before else {},
        compiler_params=params(60),
        cost_estimate=cost(4 * steps * frames * line * 256, 4 * steps * frames * line),
        name="decoded_grad",
    )(*[recon_rows] * 4, one, recon_rows, down, live, dec_cols, *before)


def decode_kernel(
    feat_ref, grad_ref, scale_ref, shift_ref, film_scale_ref, film_shift_ref,
    back_out, scale_grad_out, shift_grad_out, film_out, scale_scr, shift_grad_scr,
):
    step = pl.program_id(0)
    last = pl.num_programs(0) - 1
    channels, frames = scale_scr.shape
    line = feat_ref.shape[1]

    @pl.when(step == 0)
    def _():
        scale_scr[...] = jnp.zeros_like(scale_scr)

    scale = (scale_ref[...] * SHRINK).astype(BF)
    scaled = None
    for r in range(2):
        shift = (shift_ref[r * channels : (r + 1) * channels, :] * SHRINK).astype(BF)
        total = None
        for g in range(0, line, 4 * channels):
            backs, terms = [], []
            for j in range(g, g + 4 * channels, channels):
                rows = slice(j, j + channels)
                feat = feat_ref[r, rows, :]
                back = grad_ref[r, rows, :] * double_slope(feat * scale + shift)
                back_out[r, rows, :] = back
                backs.append(back)
                terms.append(back * feat)
            total = wide_sum(backs) if total is None else total + wide_sum(backs)
            scaled = wide_sum(terms) if scaled is None else scaled + wide_sum(terms)
        shift_grad_scr[2 * step + r] = total.astype(BF)
    scale_scr[...] += scaled

    @pl.when(step == last)
    def _():
        scale_grad = scale_scr[...].astype(BF)
        shift_grad = shift_grad_scr[...].reshape(shift_grad_out.shape)
        scale_grad_out[...] = scale_grad
        shift_grad_out[...] = shift_grad
        film_out[...] = (tn(scale_grad, film_scale_ref[...]) + tt(shift_grad, film_shift_ref[...])).astype(BF)


def decode(feat, grad, scale, shift, film_scale, film_shift):
    map_rows, line, frames = feat.shape
    channels, model = film_scale.shape
    map_spec = pl.BlockSpec((2, line, frames), lambda i: (i, 0, 0))
    grads = [
        jax.ShapeDtypeStruct((channels, frames), BF),
        jax.ShapeDtypeStruct((map_rows * channels, frames), BF),
        jax.ShapeDtypeStruct((frames, model), BF),
    ]
    return pl.pallas_call(
        decode_kernel,
        grid=(map_rows // 2,),
        in_specs=[
            map_spec,
            map_spec,
            whole(scale.shape),
            pl.BlockSpec((2 * channels, frames), lambda i: (i, 0)),
            whole(film_scale.shape),
            whole(film_shift.shape),
        ],
        out_specs=[map_spec] + [whole(g.shape) for g in grads],
        out_shape=[jax.ShapeDtypeStruct((map_rows, line, frames), BF)] + grads,
        scratch_shapes=[
            pltpu.VMEM((channels, frames), F32),
            pltpu.VMEM((map_rows, channels, frames), BF),
        ],
        compiler_params=params(60),
        cost_estimate=cost(20 * map_rows * frames * line, 6 * map_rows * frames * line, map_rows * frames * line),
        name="decode",
    )(feat, grad, scale, shift, film_scale, film_shift)


def blocks_to_lanes(values, rows):
    return jnp.concatenate([values[s : s + rows] for s in range(0, values.shape[0], rows)], axis=1)


def put(own_ref, other_ref, core, start, values):
    size, lanes = own_ref.shape[0], slice(start, start + values.shape[1])
    low = values.astype(BF)
    first = core == 0
    own_ref[:, lanes] = jnp.where(first, low[:size], low[size:])
    other_ref[:, lanes] = jnp.where(first, low[size:], low[:size])


def heads_kernel(
    place_ref, state_ref, cot_ref, live_ref, prior_ref, scale_grad_ref, shift_grad_ref, own_out, other_out,
    stream_out,
):
    live = live_ref[:, :1]
    grad = (cot_ref[...].astype(F32) * live).astype(BF)
    size = 2 * own_out.shape[0]
    core = place_ref[1]
    logits = grad.shape[1]
    state = state_ref[...]
    model = state.shape[1]
    start = pl.multiple_of(place_ref[0] * size, size)
    put(own_out, other_out, core, 0, tn(state_ref[:, pl.ds(start, size)], grad))
    stream_out[...] = nt(grad, prior_ref[...])
    scale_grad = nn(scale_grad_ref[...], state)
    blank = jnp.zeros((size - scale_grad.shape[0], model), F32)
    put(own_out, other_out, core, logits, jnp.concatenate([scale_grad, blank], axis=0))
    put(own_out, other_out, core, logits + model, blocks_to_lanes(nn(shift_grad_ref[...], state), size))


def heads(place, parts, state, logit_cot, live_cols, prior_w, scale_grad, shift_grad):
    frames, model = state.shape
    logits = logit_cot.shape[1]
    size = model // parts
    width = logits + model + shift_grad.shape[0] // size * model
    vmem = pl.BlockSpec(memory_space=pltpu.VMEM)
    return pl.pallas_call(
        heads_kernel,
        in_specs=[pl.BlockSpec(memory_space=pltpu.SMEM)] + [vmem] * 6,
        out_shape=[jax.ShapeDtypeStruct((size // 2, width), BF)] * 2
        + [jax.ShapeDtypeStruct((frames, model), F32)],
        compiler_params=params(60),
        cost_estimate=cost(4 * frames * model * logits, 4 * 1024 * 1024),
        name="heads",
    )(place, state, logit_cot, live_cols, prior_w, scale_grad, shift_grad)


def norm_backward(grad, unit, inverse):
    return (
        grad
        - jnp.mean(grad, axis=-1, keepdims=True)
        - unit * jnp.mean(grad * unit, axis=-1, keepdims=True)
    ) * inverse


def block_backward_kernel(
    columns, place_ref, part_ref, more_ref, embed_part_ref, embed_more_ref, stream_ref, ln1_ref, ln2_ref,
    down_in, slope_in, active_in, middle_in, up_in, context_in, out_in, joined_in, attend_in, qkv_in, emb_in,
    profile_in, own_out, other_out, profile_out, down_ref, slope_ref, active_ref, middle_ref, up_ref, context_ref, out_ref,
    joined_ref, attend_ref, qkv_ref, emb_ref, profile_ref, raised_scr, low_scr, grad_scr, in_sems,
):
    names = ("down", "slope", "active", "middle", "up", "context", "out", "joined", "attend", "qkv", "emb", "profile")
    sources = (
        down_in, slope_in, active_in, middle_in, up_in, context_in, out_in, joined_in, attend_in, qkv_in, emb_in,
        profile_in,
    )
    targets = (
        down_ref, slope_ref, active_ref, middle_ref, up_ref, context_ref, out_ref, joined_ref, attend_ref, qkv_ref,
        emb_ref, profile_ref,
    )
    copies = dict(zip(names, fetch(sources, targets, in_sems)))
    grad_out = stream_ref[...] + part_ref[...].astype(F32) + more_ref[...].astype(F32)
    frames, model = grad_out.shape
    hidden = up_ref.shape[1]
    branch = grad_out.astype(BF)
    place, core = place_ref[0], place_ref[1]
    size = 2 * own_out.shape[0]
    start_qkv, start_out, start_down = hidden, hidden + 3 * model, hidden + 4 * model
    start_norm = start_down + hidden // model * model
    copies["down"].wait()
    copies["slope"].wait()
    for start in range(0, hidden, 512):
        lanes = slice(start, start + 512)
        raised_scr[:, lanes] = (nt(branch, down_ref[lanes, :]) * slope_ref[:, lanes].astype(F32)).astype(BF)
    copies["active"].wait()
    for s in range(0, hidden, model):
        some = active_ref[:, pl.ds(pl.multiple_of(place * size + s, size), size)]
        put(own_out, other_out, core, start_down + s, tn(some, branch))
    copies["middle"].wait()
    middle = middle_ref[...]
    unit, inverse = normed(middle)
    low_scr[...] = (unit * ln2_ref[...]).astype(BF)
    window = pl.ds(pl.multiple_of(place * size, size), size)
    put(own_out, other_out, core, 0, tn(low_scr[:, window], raised_scr[...]))
    copies["up"].wait()
    grad = nt(raised_scr[...], up_ref[...])
    norm_two = jnp.sum(grad * unit, axis=0, keepdims=True)
    grad_middle = grad_out + norm_backward(grad * ln2_ref[...], unit, inverse)
    attended = grad_middle.astype(BF)
    copies["context"].wait()
    put(own_out, other_out, core, start_out, tn(context_ref[:, window], attended))
    copies["out"].wait()
    low_scr[...] = nt(attended, out_ref[...]).astype(BF)
    block = 128
    col = lax.broadcasted_iota(jnp.int32, (block, block), 1)
    first = col < 64
    scaling = 1.0 / math.sqrt(model // HEADS)
    copies["joined"].wait()
    copies["attend"].wait()
    for b in range(frames // block):
        part = slice(b * block, (b + 1) * block)
        for pair in range(HEADS // 2):
            lanes = pair * 128
            queries = joined_ref[part, lanes : lanes + 128]
            keys = stacked_heads(joined_ref[part, model + lanes : model + lanes + 128], col)
            values = stacked_heads(joined_ref[part, 2 * model + lanes : 2 * model + lanes + 128], col)
            grads = low_scr[part, lanes : lanes + 128]
            weights_low = attend_ref[b * HEADS // 2 + pair]
            weights = weights_low.astype(F32)
            terms = weights * nt(grads, values)
            halves = []
            for half in range(2):
                some = slice(half * block, (half + 1) * block)
                inner = jnp.sum(terms[:, some], axis=-1, keepdims=True)
                halves.append((terms[:, some] - weights[:, some] * inner).astype(BF))
            grad_scores = jnp.concatenate(halves, axis=1)
            grad_queries = nn(grad_scores, keys)
            both = tn(grad_scores, queries)
            grad_keys = jnp.where(first, both[:block], both[block:])
            both = tn(weights_low, grads)
            grad_values = jnp.where(first, both[:block], both[block:])
            for k, term in enumerate((grad_queries * scaling, grad_keys * scaling, grad_values)):
                grad_scr[part, k * model + lanes : k * model + lanes + 128] = term.astype(BF)
    unit, inverse = normed(embed_part_ref[...].astype(F32) + embed_more_ref[...].astype(F32))
    low_scr[...] = (unit * ln1_ref[...]).astype(BF)
    put(own_out, other_out, core, start_qkv, tn(low_scr[:, window], grad_scr[...]))
    copies["qkv"].wait()
    grad = nt(grad_scr[...], qkv_ref[...])
    norm_one = jnp.sum(grad * unit, axis=0, keepdims=True)
    lines = [norm[:, s : s + 128] for norm in (norm_one, norm_two) for s in range(0, model, 128)]
    lines.append(jnp.zeros((size - len(lines), 128), F32))
    put(own_out, other_out, core, start_norm, jnp.concatenate(lines, axis=0))
    grad_embed = (grad_middle + norm_backward(grad * ln1_ref[...], unit, inverse)).astype(BF)
    copies["emb"].wait()
    profile_out[...] = nt(emb_ref[...], grad_embed) * (1.0 / columns)
    copies["profile"].wait()
    put(own_out, other_out, core, start_norm + 128, blocks_to_lanes(nn(profile_ref[...], grad_embed), size))


def block_backward(
    columns, parts, place, grads, embeds, stream, joined, attend, context, middle, active, slope, profile,
    ln1, qkv, out_w, ln2, up_w, down_w, emb,
):
    frames, model = stream.shape
    hidden = up_w.shape[1]
    size = model // parts
    width = 2 * hidden + 4 * model + 128 + emb.shape[0] // size * model
    shapes = [((size // 2, width), BF), ((size // 2, width), BF), (profile.shape, F32)]
    vmem, hbm = pl.BlockSpec(memory_space=pltpu.VMEM), pl.BlockSpec(memory_space=pl.ANY)
    near = (*grads, *embeds, stream, ln1, ln2)
    staged = (down_w, slope, active, middle, up_w, context, out_w, joined, attend, qkv, emb, profile)
    return pl.pallas_call(
        functools.partial(block_backward_kernel, columns),
        in_specs=[pl.BlockSpec(memory_space=pltpu.SMEM)] + [vmem] * len(near) + [hbm] * len(staged),
        out_shape=[jax.ShapeDtypeStruct(*s) for s in shapes],
        scratch_shapes=[pltpu.VMEM(x.shape, x.dtype) for x in staged]
        + [
            pltpu.VMEM((frames, hidden), BF),
            pltpu.VMEM((frames, model), BF),
            pltpu.VMEM((frames, 3 * model), BF),
            pltpu.SemaphoreType.DMA((len(staged),)),
        ],
        compiler_params=params(60),
        cost_estimate=cost(3 * frames * model * (4 * model + 2 * hidden), 20 * 1024 * 1024),
        name="block_backward",
    )(place, *near, *staged)


def scatter_body(
    step, last, row_refs, first_ref, up_ref, down_ref, live, matrix_ref, places_ref, outs, scrs, fill
):
    rows_out, rim_up_out, rim_down_out, taps_out = outs
    ring_scr, window_scr, low_scr, rows_scr, held_scr, cov_scr = scrs
    _, lanes, frames = up_ref.shape
    depth, _ = matrix_ref.shape
    stride = lanes // GROUPS
    inner = slice(PAD, PAD + lanes)
    kind = rows_out.dtype

    @pl.when(step == 0)
    def _():
        cov_scr[...] = jnp.zeros_like(cov_scr)
        rows_scr[...] = jnp.zeros_like(rows_scr)
        held_scr[...] = jnp.zeros_like(held_scr)

    rows_out[0:3] = held_scr[...]

    @pl.when(step < last)
    def _():
        fill_six(
            ring_scr, step == 0, step == last - 1, (lambda: up_ref[0], lambda: first_ref[0]), row_refs, down_ref,
            live,
        )
        matrix = matrix_ref[...]
        for r in range(2):
            fill_windows_at(window_scr, ring_scr, 2 * r, depth // SLOT, stride)
            fill(r)
            placed = nn(matrix, low_scr[...])
            for g in range(GROUPS):
                add_rows(rows_scr, 2 * r, placed[:, g * frames : (g + 1) * frames], g, stride)
            cov_scr[...] += nt(low_scr[...], window_scr[...])

    rows_out[3] = rows_scr[0, inner, :].astype(kind)

    @pl.when(step == 0)
    def _():
        rim_up_out[...] = rows_scr[0, inner, :].astype(BF)

    @pl.when(step == last)
    def _():
        rim_down_out[...] = rows_scr[1, inner, :].astype(BF)
        taps_out[...] = fold_taps(cov_scr, places_ref, taps_out.shape[1])

    @pl.when(step < last)
    def _():
        held_scr[...] = rows_scr[1:4, inner, :].astype(kind)
        rows_scr[0:2] = rows_scr[4:6]
        rows_scr[2:6] = jnp.zeros((4,) + rows_scr.shape[1:], F32)


def rebuild_kernel(
    feat_ref, a_ref, b_ref, c_ref, d_ref, first_ref, up_ref, down_ref, live_ref, dec_ref, scale_ref, shift_ref,
    places_ref, rows_out, rim_up_out, rim_down_out, taps_out,
    ring_scr, window_scr, low_scr, rows_scr, held_scr, cov_scr,
):
    frames = up_ref.shape[2]
    width = dec_ref.shape[1]
    channels = scale_ref.shape[0]

    def fill(r):
        scale = (scale_ref[...] * 0.5).astype(BF)
        shift = (shift_ref[r * channels : (r + 1) * channels, :] * 0.5).astype(BF)
        for g in range(GROUPS):
            for tile, column in tiles(frames, g):
                for j in range(0, width, channels):
                    feat = feat_ref[r, g * width + j : g * width + j + channels, tile]
                    low_scr[j : j + channels, column] = gelu_of_half(feat * scale[:, tile] + shift[:, tile])

    scatter_body(
        pl.program_id(0), pl.num_programs(0) - 1, (a_ref, b_ref, c_ref, d_ref), first_ref, up_ref, down_ref,
        live_ref[...], dec_ref, places_ref, (rows_out, rim_up_out, rim_down_out, taps_out),
        (ring_scr, window_scr, low_scr, rows_scr, held_scr, cov_scr), fill,
    )


def encode_backward_kernel(
    back_ref, a_ref, b_ref, c_ref, d_ref, first_ref, up_ref, down_ref, enc_cols_ref, enc_ref, scale_ref, profile_ref,
    places_ref, rows_out, rim_up_out, rim_down_out, taps_out,
    ring_scr, window_scr, low_scr, rows_scr, held_scr, cov_scr, value_scr,
):
    frames = up_ref.shape[2]
    width = enc_ref.shape[1]
    channels = scale_ref.shape[0]

    def fill(r):
        value_scr[...] = nn(enc_cols_ref[...], window_scr[...])
        scale = (scale_ref[...] * 0.5).astype(BF)
        mean = (profile_ref[r * channels : (r + 1) * channels, :] * 0.5).astype(BF)
        for g in range(GROUPS):
            for tile, column in tiles(frames, g):
                for j in range(0, width, channels):
                    back = back_ref[r, g * width + j : g * width + j + channels, tile]
                    slope = double_slope((value_scr[j : j + channels, column] * SHRINK).astype(BF))
                    low_scr[j : j + channels, column] = (back * scale[:, tile] + mean[:, tile]) * slope

    scatter_body(
        pl.program_id(0), pl.num_programs(0) - 1, (a_ref, b_ref, c_ref, d_ref), first_ref, up_ref, down_ref,
        None, enc_ref, places_ref, (rows_out, rim_up_out, rim_down_out, taps_out),
        (ring_scr, window_scr, low_scr, rows_scr, held_scr, cov_scr), fill,
    )


def scatter_call(kernel, name, kind, which, map_in, rows_in, up, down, more, more_specs, width, depth, channels):
    rows, lanes, frames = rows_in.shape
    steps = rows // 4
    line = GROUPS * width
    rim = jax.ShapeDtypeStruct((lanes, frames), BF)
    taps = jax.ShapeDtypeStruct((more[-1].shape[1], channels), F32)
    scratch = [
        pltpu.VMEM((6, lanes + 2 * PAD, frames), BF),
        pltpu.VMEM((depth, GROUPS * frames), BF),
        pltpu.VMEM((width, GROUPS * frames), BF),
        pltpu.VMEM((6, lanes + 2 * PAD, frames), F32),
        pltpu.VMEM((3, lanes, frames), kind),
        pltpu.VMEM((width, depth), F32),
    ]
    if which == 0:
        scratch.append(pltpu.VMEM((width, GROUPS * frames), F32))
    return pl.pallas_call(
        kernel,
        grid=(steps + 1,),
        in_specs=[pl.BlockSpec((2, line, frames), lambda i: (jnp.minimum(i, steps - 1), 0, 0))]
        + four_row_specs(frames, lanes, rows)
        + [pl.BlockSpec((1, lanes, frames), lambda i: (0, 0, 0)), halo_spec(up, which), halo_spec(down, which)]
        + more_specs,
        out_specs=[
            pl.BlockSpec((4, lanes, frames), lambda i: (jnp.maximum(i - 1, 0), 0, 0)),
            whole(rim.shape),
            whole(rim.shape),
            whole(taps.shape),
        ],
        out_shape=[jax.ShapeDtypeStruct((rows, lanes, frames), kind), rim, rim, taps],
        scratch_shapes=scratch,
        compiler_params=params(60),
        cost_estimate=cost(4 * rows * frames * line * 128, 2 * rows * frames * line),
        name=name,
    )(map_in, *[rows_in] * 5, up, down, *more)


def row_block(channels, frames, rows):
    return pl.BlockSpec((2 * channels, frames), lambda i: (jnp.minimum(i, rows // 4 - 1), 0))


def rebuild(feat, recon_rows, up, down, live, dec, scale, shift, places):
    rows, _, frames = recon_rows.shape
    channels = scale.shape[0]
    return scatter_call(
        rebuild_kernel, "rebuild", BF, 1, feat, recon_rows, up, down, (live, dec, scale, shift, places),
        [whole(live.shape), whole(dec.shape), whole(scale.shape), row_block(channels, frames, rows), whole(places.shape)],
        dec.shape[1], dec.shape[0], channels,
    )


def encode_backward(back, image_rows, up, down, enc_cols, enc, scale, profile, places):
    rows, _, frames = image_rows.shape
    channels = scale.shape[0]
    return scatter_call(
        encode_backward_kernel, "encode_backward", F32, 0, back, image_rows, up, down,
        (enc_cols, enc, scale, profile, places),
        [
            whole(enc_cols.shape), whole(enc.shape), whole(scale.shape), row_block(channels, frames, rows),
            whole(places.shape),
        ],
        enc.shape[1], enc.shape[0], channels,
    )


def rims_kernel(low_ref, wide_ref, above_ref, below_ref, low_out, wide_out):
    for at, rim_ref in ((0, above_ref), (1, below_ref)):

        @pl.when(pl.program_id(0) == at)
        def _(rim_ref=rim_ref):
            for k, (rows_ref, out_ref) in enumerate(((low_ref, low_out), (wide_ref, wide_out))):
                out_ref[0] = (rows_ref[0].astype(F32) + rim_ref[k].astype(F32)).astype(out_ref.dtype)


def with_rims(low, wide, above, below):
    count, lanes, frames = low.shape
    row_spec = pl.BlockSpec((1, lanes, frames), lambda i: (i * (count - 1), 0, 0))
    return pl.pallas_call(
        rims_kernel,
        grid=(2,),
        in_specs=[row_spec, row_spec, whole(above.shape), whole(below.shape)],
        out_specs=[row_spec, row_spec],
        out_shape=[jax.ShapeDtypeStruct(low.shape, low.dtype), jax.ShapeDtypeStruct(wide.shape, wide.dtype)],
        input_output_aliases={0: 0, 1: 1},
        compiler_params=params(60),
        cost_estimate=cost(0, 16 * lanes * frames),
        name="with_rims",
    )(low, wide, above, below)


def send_along(values, axis, step):
    count = lax.axis_size(axis)
    pairs = [(i, i + step) for i in range(count) if 0 <= i + step < count]
    return lax.ppermute(values, axis, pairs)


def swap(values, axis, distance):
    count = lax.axis_size(axis)
    return lax.ppermute(values, axis, [(i, i ^ distance) for i in range(count)])


def cross(values, turn):
    rows, frames = lax.axis_size("rows"), lax.axis_size("frames")
    pairs = []
    for r in range(rows):
        for f in range(frames):
            distance = 1 + (f + turn) % 2
            pairs.append((r * frames + f, (r ^ distance) * frames + f))
    return lax.ppermute(values, ("rows", "frames"), pairs)


def add(values, more):
    return (values.astype(F32) + more.astype(F32)).astype(BF)


def chip_groups():
    count = lax.axis_size("frames")
    return [list(range(core, count, 2)) for core in range(2)]


def split_over(values, groups):
    count = len(groups[0])
    split = values.reshape((count, values.shape[0] // count) + values.shape[1:])
    return lax.all_to_all(split, "frames", 0, 0, axis_index_groups=groups)


def sum_parts(parts):
    return jnp.sum(parts.astype(F32), axis=0).astype(BF)


def gather_over(values, axis):
    count = lax.axis_size(axis)
    copies = jnp.broadcast_to(values[None], (count,) + values.shape)
    return lax.all_to_all(copies, axis, 0, 0)


def swap_frames(values, distance):
    count = lax.axis_size("frames")
    return lax.ppermute(values, "frames", [(f, f ^ distance) for f in range(count)])


def gather_chips(values):
    count = lax.axis_size("frames") // 2
    copies = jnp.broadcast_to(values[None], (count,) + values.shape)
    return lax.all_to_all(copies, "frames", 0, 0, axis_index_groups=chip_groups())


def finish_kernel(slots, widths, place_ref, *refs):
    count = len(slots)
    own_in, other_in = refs[:count], refs[count : 2 * count]
    outs, (own_scr, other_scr, sems) = refs[-10:-3], refs[-3:]
    scale_before = refs[-11]
    step = pl.program_id(0)
    core = place_ref[4]
    chips = own_scr.shape[1]
    copies = [
        [pltpu.make_async_copy(ref, scr.at[k], sems.at[side, k]) for k, ref in enumerate(sources)]
        for side, (sources, scr) in enumerate(((own_in, own_scr), (other_in, other_scr)))
    ]

    @pl.when(step == 0)
    def _():
        for k in range(count):
            copies[0][k].start()
            copies[1][k].start()

    for k in range(count):

        @pl.when(step == k)
        def _(k=k):
            copies[0][k].wait()
            copies[1][k].wait()
            for scr, half in ((own_scr, core), (other_scr, 1 - core)):
                for chip in range(chips):
                    at, piece = 0, half * chips + chip
                    for out, (kind, lanes) in zip(outs, widths):
                        part = scr[k, chip, :, at : at + lanes].astype(F32)
                        at += lanes
                        if kind == "row":
                            out[piece] = part
                        elif kind == "blocks":
                            size = out.shape[-1]
                            for block in range(out.shape[0]):
                                out[block, piece] = part[:, block * size : (block + 1) * size]
                        elif kind == "norm" and k == 0:
                            out[piece] = part
                        elif kind == "scale":
                            if k:
                                out[piece] += part
                            else:
                                out[piece] = part + scale_before[piece] if slots[0] else part


def finish(place, slots, own, other, before, logits, model, hidden):
    chips, size, lanes = own[0].shape
    pieces = 2 * chips
    quarters = 4
    many = hidden // model
    widths = (
        ("row", logits), ("scale", model), ("row", hidden), ("row", 3 * model), ("row", model), ("blocks", hidden),
        ("norm", 128),
    )
    specs, shapes = [], []
    for kind, width in widths:
        if kind == "blocks":
            shape, index = (many, pieces, size, model), lambda k, place: (0, place[slots[0] + k], 0, 0)
            shapes.append((many, quarters * pieces, size, model))
        elif kind == "row":
            shape, index = (pieces, size, width), lambda k, place: (place[slots[0] + k], 0, 0)
            shapes.append((quarters * pieces, size, width))
        else:
            shape, index = (pieces, size, width), lambda k, place: (0, 0, 0)
            shapes.append(shape)
        specs.append(pl.BlockSpec(shape, index))
    held = pltpu.VMEM((len(slots), chips, size, lanes), BF)
    arrays = len(own) + len(other)
    kept = [k for k, (kind, _) in enumerate(widths) if kind in ("row", "blocks")]
    more = [before[k] for k in kept] + [before[1]] if before else [jnp.zeros((1, 8, 128), F32)]
    return pl.pallas_call(
        functools.partial(finish_kernel, slots, widths),
        grid_spec=pltpu.PrefetchScalarGridSpec(
            num_scalar_prefetch=1,
            grid=(len(slots),),
            in_specs=[pl.BlockSpec(memory_space=pl.ANY)] * (arrays + len(more) - 1) + [whole(more[-1].shape)],
            out_specs=specs,
            scratch_shapes=[held, held, pltpu.SemaphoreType.DMA((2, len(slots)))],
        ),
        out_shape=[jax.ShapeDtypeStruct(shape, F32) for shape in shapes],
        input_output_aliases={1 + arrays + n: k for n, k in enumerate(kept)} if before else {},
        compiler_params=params(60),
        cost_estimate=cost(0, 10 * len(slots) * own[0].size),
        name="finish",
    )(place, *own, *other, *more)


def split_finish_kernel(place_ref, split_ref, split_other_ref, *outs):
    core = place_ref[4]
    chips = split_ref.shape[0]
    pieces = 2 * chips
    for ref, half in ((split_ref, core), (split_other_ref, 1 - core)):
        for chip in range(chips):
            at = 0
            for out in outs:
                lanes = out.shape[-1]
                for block in range(out.shape[0] // pieces):
                    out[block * pieces + half * chips + chip] = ref[chip, :, at : at + lanes].astype(F32)
                    at += lanes


def split_finish(place, split, split_other, model):
    chips, size, lanes = split.shape
    shape = (lanes // (2 * model) * 2 * chips, size, model)
    vmem = pl.BlockSpec(memory_space=pltpu.VMEM)
    return pl.pallas_call(
        split_finish_kernel,
        in_specs=[pl.BlockSpec(memory_space=pltpu.SMEM), vmem, vmem],
        out_shape=[jax.ShapeDtypeStruct(shape, F32)] * 2,
        compiler_params=params(40),
        cost_estimate=cost(0, 8 * split.size),
        name="split_finish",
    )(place, split, split_other)


def on_device(
    images, enc_kernel, emb_weight, ln1_gain, qkv_weight, out_weight, ln2_gain, up_weight, down_weight,
    prior_weight, film_scale, film_shift, dec_kernel, horizons, frame_valid, recon_cot, logit_cot,
):
    frames, rows, lanes = images.shape
    taps, _, chan_in, channels = enc_kernel.shape
    columns = lanes // chan_in // 2
    copies = columns // GROUPS
    model = qkv_weight.shape[0]
    hidden = up_weight.shape[1]
    slots = frames // horizons.shape[0]
    count = lax.axis_size("rows")

    places = jnp.asarray(tap_places(taps, chan_in, copies), BF)
    enc_taps = jnp.transpose(enc_kernel, (0, 2, 1, 3)).reshape(taps * chan_in * taps, channels)
    dec_taps = jnp.transpose(dec_kernel, (0, 3, 1, 2)).reshape(taps * chan_in * taps, channels)
    film_scale_rows = film_scale.T
    image_rows = jnp.transpose(images, (1, 2, 0))
    recon_rows = jnp.transpose(recon_cot, (1, 2, 0))

    steps = jnp.arange(slots)
    reached = (steps[None, :] <= horizons[:, None]).reshape(frames)
    live = (reached & (frame_valid > 0)).astype(F32)
    live_cols = jnp.broadcast_to(live[:, None], (frames, 128))
    keys_ok = reached.astype(F32)[None, :]
    place = jnp.stack([lax.axis_index("rows"), lax.axis_index("frames") % 2]).astype(jnp.int32)

    above = send_along(jnp.stack([image_rows[-1], recon_rows[-1]]), "rows", 1)
    below = send_along(jnp.stack([image_rows[0], recon_rows[0]]), "rows", -1)
    enc_cols, enc, dec_cols, dec = expand(enc_taps, dec_taps, places)

    feat, inner = encode_inner(image_rows, enc_cols, channels)
    feat, profile, embed_part = encode_edge(image_rows, above, below, enc_cols, emb_weight, inner, feat)
    recon_later, embed_part = lax.optimization_barrier((recon_rows, embed_part))
    embed_more = cross(embed_part, 0)
    half = rows // 8
    decoded_args = (recon_later, above, below, live[None, :], dec_cols)
    grad = decoded_grad(*decoded_args, 0, half, ())
    embed_more, grad = lax.optimization_barrier((embed_more, grad))
    embed_part = add(embed_part, embed_more)
    embed_more = cross(embed_part, 1)
    grad = decoded_grad(*decoded_args, half, rows // 4 - half, (grad,))
    embed_more, grad = lax.optimization_barrier((embed_more, grad))
    embeds = embed_part, embed_more
    joined, attend, context, middle, active, active_slope, state, scale, shift = block_forward(
        slots, embeds, keys_ok, ln1_gain[None], qkv_weight, out_weight, ln2_gain[None], up_weight, down_weight,
        film_scale_rows, film_shift,
    )
    back, scale_grad, shift_grad, film_part = decode(feat, grad, scale, shift, film_scale_rows, film_shift)
    film_more = cross(film_part, 0)
    head_own, head_other, stream = heads(place, count, state, logit_cot, live_cols, prior_weight, scale_grad, shift_grad)
    film_more, head_other = lax.optimization_barrier((film_more, head_other))
    film_part = add(film_part, film_more)
    film_more = cross(film_part, 1)
    head_half_sum = add(head_own, swap_frames(head_other, 1))
    film_more, head_half_sum = lax.optimization_barrier((film_more, head_half_sum))
    head_parts = split_over(head_half_sum, chip_groups())
    block_own, block_other, grad_profile = block_backward(
        columns, count, place, (film_part, film_more), embeds, stream, joined, attend, context, middle, active,
        active_slope, profile, ln1_gain[None], qkv_weight, out_weight, ln2_gain[None], up_weight, down_weight,
        emb_weight,
    )
    head_parts, block_other = lax.optimization_barrier((head_parts, block_other))
    head_piece = sum_parts(head_parts)
    logits = prior_weight.shape[1]
    head_lanes, block_lanes = logits + model, 2 * hidden + 4 * model + 128
    block_more = swap_frames(block_other, 1)
    block_half_sum = add(block_own, block_more)
    feat, block_half_sum = lax.optimization_barrier((feat, block_half_sum))
    block_parts = split_over(block_half_sum, chip_groups())
    rebuilt_rows, rim_up, rim_down, dec_cov = rebuild(
        feat, recon_rows, above, below, live[None, :], dec, scale, shift, places
    )
    block_parts, dec_cov = lax.optimization_barrier((block_parts, dec_cov))
    block_piece = sum_parts(block_parts)
    shared = jnp.concatenate([head_piece[:, :head_lanes], block_piece[:, :block_lanes]], axis=1)
    shared, back = lax.optimization_barrier((shared, back))
    own = gather_chips(shared)
    image_grad, image_up, image_down, enc_cov = encode_backward(
        back, image_rows, above, below, enc_cols, enc, scale, grad_profile, places
    )
    own, enc_cov = lax.optimization_barrier((own, enc_cov))
    near, far, own_other = cross(own, 0), cross(own, 1), swap_frames(own, 1)
    covs = jnp.concatenate([enc_cov, dec_cov], axis=1)
    step = lax.axis_size("frames") // 2
    while step:
        covs = covs + swap_frames(covs, step)
        step //= 2
    row, core = lax.axis_index("rows"), lax.axis_index("frames") % 2
    slots_of = jnp.stack([row, row ^ (1 + core), row ^ (2 - core), row ^ 3, core]).astype(jnp.int32)
    split = gather_chips(jnp.concatenate([head_piece[:, head_lanes:], block_piece[:, block_lanes:]], axis=1))
    near, far, own_other, covs, split = lax.optimization_barrier((near, far, own_other, covs, split))
    both = cross(near, 1)
    near_other, far_other = swap_frames(near, 1), swap_frames(far, 1)
    found = finish(
        slots_of, (0, 1, 2), (own, near, far), (own_other, far_other, near_other), (), logits, model, hidden
    )
    film_shift_grad, emb_grad = split_finish(slots_of, split, swap_frames(split, 1), model)
    film_shift_grad = film_shift_grad.reshape(-1, model).T
    emb_grad = emb_grad.reshape(-1, model)
    norm_grads = found[6].reshape(-1, 128)[: 2 * model // 128].reshape(2, model)
    rims = jnp.stack([rim_down, image_down]), jnp.stack([rim_up, image_up])
    both, covs, rims, film_shift_grad, emb_grad, norm_grads, *found = lax.optimization_barrier(
        (both, covs, rims, film_shift_grad, emb_grad, norm_grads, *found)
    )
    both_other = swap_frames(both, 1)
    rims_above, rims_below = send_along(rims[0], "rows", 1), send_along(rims[1], "rows", -1)
    for distance in (1, 2):
        covs = covs + lax.ppermute(covs, "rows", [(r, r ^ distance) for r in range(count)])
    found = finish(slots_of, (3,), (both,), (both_other,), found, logits, model, hidden)
    prior_grad, misc, up_grad, qkv_grad, out_grad, down_grad = [
        array.reshape(-1, array.shape[-1]) for array in found[:6]
    ]
    film_scale_grad = misc[:channels].T
    rims_above, rims_below, film_scale_grad, prior_grad = lax.optimization_barrier(
        (rims_above, rims_below, film_scale_grad, prior_grad)
    )
    rebuilt_rows, image_grad = with_rims(rebuilt_rows, image_grad, rims_above, rims_below)
    enc_cov, dec_cov = covs[:, :channels], covs[:, channels:]
    enc_grad = jnp.transpose(enc_cov.reshape(taps, chan_in, taps, channels), (0, 2, 1, 3))
    dec_grad = jnp.transpose(dec_cov.reshape(taps, chan_in, taps, channels), (0, 2, 3, 1))
    return (
        jnp.transpose(rebuilt_rows, (2, 0, 1)),
        jnp.transpose(image_grad, (2, 0, 1)),
        enc_grad,
        emb_grad,
        norm_grads[0],
        qkv_grad,
        out_grad,
        norm_grads[1],
        up_grad,
        down_grad,
        prior_grad,
        film_scale_grad,
        film_shift_grad,
        dec_grad,
    )


def solution(mesh):
    return jax.shard_map(
        on_device,
        mesh=mesh,
        in_specs=(
            P("frames", "rows", None),
            P(),
            P("rows", None),
            P(),
            P(),
            P(),
            P(),
            P(),
            P(),
            P(),
            P(),
            P(None, "rows"),
            P(),
            P("frames"),
            P("frames"),
            P("frames", "rows", None),
            P("frames", None),
        ),
        out_specs=(
            P("frames", "rows", None),
            P("frames", "rows", None),
            P(),
            P("rows", None),
            P(),
            P(),
            P(),
            P(),
            P(),
            P(),
            P(),
            P(),
            P(None, "rows"),
            P(),
        ),
        check_vma=False,
    )
```

```python
import functools
import math

import jax
import jax.numpy as jnp
import numpy as np
from jax import lax
from jax.experimental import pallas as pl
from jax.experimental.pallas import tpu as pltpu
from jax.sharding import PartitionSpec as P

HEADS = 8
BF = jnp.bfloat16
F32 = jnp.float32
GROUPS = 4
SLOT = 64
PAD = 8
TILE = 384
ROOT = math.sqrt(2.0 / math.pi)
CUBE = 0.044715
MIB = 1024 * 1024


def nn(lhs, rhs):
    return lax.dot_general(lhs, rhs, (((1,), (0,)), ((), ())), preferred_element_type=F32)


def nt(lhs, rhs):
    return lax.dot_general(lhs, rhs, (((1,), (1,)), ((), ())), preferred_element_type=F32)


def tn(lhs, rhs):
    return lax.dot_general(lhs, rhs, (((0,), (0,)), ((), ())), preferred_element_type=F32)


def tt(lhs, rhs):
    return lax.dot_general(lhs, rhs, (((0,), (1,)), ((), ())), preferred_element_type=F32)


SHRINK = (ROOT * CUBE) ** (1.0 / 3.0)
BEND = ROOT / SHRINK


def gelu_of_half(half):
    bend = half * ((8.0 * ROOT * CUBE) * (half * half) + 2.0 * ROOT)
    return half * (jnp.tanh(bend.astype(F32)) + 1.0).astype(BF)


def double_slope(shrunk):
    square = shrunk * shrunk
    bend = shrunk * (square + BEND)
    level = jnp.tanh(bend.astype(F32))
    rise, fall = (1.0 + level).astype(BF), (1.0 - level).astype(BF)
    return rise * (shrunk * (3.0 * square + BEND) * fall + 1.0)


def gelu_pair(value):
    square = value * value
    bend = (ROOT * CUBE) * square + ROOT
    gate = 0.5 * jnp.tanh(value * bend) + 0.5
    result = value * gate
    slope = gate + result * (1.0 - gate) * ((6.0 * ROOT * CUBE) * square + 2.0 * ROOT)
    return result, slope


def wide_sum(parts):
    total = None
    for k in range(0, len(parts), 4):
        some = parts[k : k + 4]
        while len(some) > 1:
            some = [a + b for a, b in zip(some[::2], some[1::2])]
        total = some[0].astype(F32) if total is None else total + some[0].astype(F32)
    return total


def whole(shape):
    return pl.BlockSpec(shape, lambda *_: (0,) * len(shape))


def params(mib):
    return pltpu.CompilerParams(vmem_limit_bytes=mib * MIB)


def cost(flops, nbytes, transcendentals=0):
    return pl.CostEstimate(flops=flops, bytes_accessed=nbytes, transcendentals=transcendentals)


def tap_places(taps, chan_in, copies):
    places = np.zeros((copies, taps * chan_in * taps, taps * SLOT), np.float32)
    for j in range(copies):
        for kh in range(taps):
            for c in range(chan_in):
                for kw in range(taps):
                    place = PAD - chan_in + (2 * j + kw) * chan_in + c
                    places[j, (kh * chan_in + c) * taps + kw, kh * SLOT + place] = 1.0
    return places


def expand_kernel(enc_ref, dec_ref, places_ref, enc_cols_out, enc_out, dec_cols_out, dec_out):
    for source, cols, out in ((enc_ref, enc_cols_out, enc_out), (dec_ref, dec_cols_out, dec_out)):
        taps = source[...]
        spread = jnp.concatenate([tn(taps, places_ref[j]) for j in range(places_ref.shape[0])], axis=0)
        cols[...] = spread.astype(BF)
        out[...] = jnp.transpose(spread).astype(BF)


def expand(enc_taps, dec_taps, places):
    copies, channels, size = places.shape
    width = copies * enc_taps.shape[1]
    cols = jax.ShapeDtypeStruct((width, size), BF)
    rows = jax.ShapeDtypeStruct((size, width), BF)
    return pl.pallas_call(
        expand_kernel,
        out_shape=[cols, rows, cols, rows],
        compiler_params=params(60),
        name="expand",
    )(enc_taps, dec_taps, places)


def keep_row(ring_ref, slot, row):
    ring_ref[slot, PAD : PAD + row.shape[0], :] = row


def window(ring_ref, first, taps, g, stride):
    return jnp.concatenate(
        [ring_ref[lax.rem(first + kh, 4), g * stride : g * stride + SLOT, :] for kh in range(taps)], axis=0
    )


def fold_taps(cov_ref, places_ref, channels):
    total = None
    for j in range(places_ref.shape[0]):
        term = lax.dot_general(
            places_ref[j].astype(F32),
            cov_ref[j * channels : (j + 1) * channels, :],
            (((1,), (1,)), ((), ())),
            precision=lax.Precision.HIGHEST,
            preferred_element_type=F32,
        )
        total = term if total is None else total + term
    return total


def halo_spec(halo, which):
    return pl.BlockSpec((1,) + halo.shape[1:], lambda i: (which, 0, 0))


def four_row_specs(frames, lanes, rows, base=0):
    return [
        pl.BlockSpec((1, lanes, frames), lambda i, k=k: (jnp.minimum(4 * (i + base) + k, rows - 1), 0, 0))
        for k in range(1, 5)
    ]


def fill_six(ring_scr, first, last, start, row_refs, down_ref, live=None):
    def masked(row):
        return row if live is None else (row.astype(F32) * live).astype(BF)

    @pl.when(first)
    def _():
        ring_scr[...] = jnp.zeros_like(ring_scr)
        for slot, row in enumerate(start):
            keep_row(ring_scr, slot, masked(row()))

    @pl.when(jnp.logical_not(first))
    def _():
        ring_scr[0:2] = ring_scr[4:6]

    for k, ref in enumerate(row_refs[:3]):
        keep_row(ring_scr, k + 2, masked(ref[0]))

    @pl.when(jnp.logical_not(last))
    def _():
        keep_row(ring_scr, 5, masked(row_refs[3][0]))

    @pl.when(last)
    def _():
        keep_row(ring_scr, 5, masked(down_ref[0]))


def fill_windows_at(window_scr, ring_scr, first, taps, stride):
    frames = ring_scr.shape[2]
    for g in range(GROUPS):
        for kh in range(taps):
            window_scr[kh * SLOT : (kh + 1) * SLOT, g * frames : (g + 1) * frames] = ring_scr[
                first + kh, g * stride : g * stride + SLOT, :
            ]


def add_rows(rows_scr, first, placed, g, stride):
    for kh in range(placed.shape[0] // SLOT):
        part = slice(g * stride, g * stride + SLOT)
        rows_scr[first + kh, part, :] += placed[kh * SLOT : (kh + 1) * SLOT, :]


def fill_windows(window_scr, ring_scr, first, taps, stride):
    frames = ring_scr.shape[2]
    for g in range(GROUPS):
        window_scr[:, g * frames : (g + 1) * frames] = window(ring_scr, first, taps, g, stride)


def tiles(frames, g):
    size = min(TILE, frames)
    return [(slice(t, t + size), slice(g * frames + t, g * frames + t + size)) for t in range(0, frames, size)]


def encode_row(ring_scr, first, enc_ref, feat_out, window_scr, value_scr, sum_scr, stride):
    width, depth = enc_ref.shape
    channels, frames = sum_scr.shape
    fill_windows(window_scr, ring_scr, first, depth // SLOT, stride)
    value_scr[...] = nn(enc_ref[...] * 0.5, window_scr[...])
    for g in range(GROUPS):
        for tile, column in tiles(frames, g):
            found = []
            for j in range(0, width, channels):
                low = gelu_of_half(value_scr[j : j + channels, column].astype(BF))
                feat_out[0, g * width + j : g * width + j + channels, tile] = low
                found.append(low)
            sum_scr[:, tile] = wide_sum(found) if g == 0 else sum_scr[:, tile] + wide_sum(found)
    return (sum_scr[...] * (1.0 / (GROUPS * width // channels))).astype(BF)


def encode_inner_kernel(
    odd_ref, even_ref, one_ref, two_ref, enc_ref, feat_out, profile_out, ring_scr, window_scr, value_scr, sum_scr
):
    step = pl.program_id(0)

    @pl.when(step == 0)
    def _():
        ring_scr[...] = jnp.zeros_like(ring_scr)
        keep_row(ring_scr, 2, one_ref[0])
        keep_row(ring_scr, 3, two_ref[0])

    keep_row(ring_scr, lax.rem(2 * step, 4), odd_ref[0])
    keep_row(ring_scr, lax.rem(2 * step + 1, 4), even_ref[0])
    stride = odd_ref.shape[1] // GROUPS
    profile_out[...] = encode_row(
        ring_scr, 2 * step + 2, enc_ref, feat_out, window_scr, value_scr, sum_scr, stride
    )


def encode_edge_kernel(
    a_ref, b_ref, c_ref, up_ref, down_ref, enc_ref, emb_ref, inner_ref, feat_ref,
    feat_out, profile_out, embed_out, ring_scr, window_scr, value_scr, sum_scr,
):
    del feat_ref
    step = pl.program_id(0)
    channels = sum_scr.shape[0]

    @pl.when(step == 0)
    def _():
        ring_scr[...] = jnp.zeros_like(ring_scr)
        keep_row(ring_scr, 0, up_ref[0])
        for k, ref in enumerate((a_ref, b_ref, c_ref)):
            keep_row(ring_scr, k + 1, ref[0])

    @pl.when(step == 1)
    def _():
        for k, ref in enumerate((a_ref, b_ref, c_ref)):
            keep_row(ring_scr, k, ref[0])
        keep_row(ring_scr, 3, down_ref[0])

    stride = up_ref.shape[1] // GROUPS
    profile = encode_row(ring_scr, 0, enc_ref, feat_out, window_scr, value_scr, sum_scr, stride)
    size = profile_out.shape[0]

    @pl.when(step == 0)
    def _():
        profile_out[:channels, :] = profile
        profile_out[channels : size - channels, :] = inner_ref[...]

    @pl.when(step == 1)
    def _():
        profile_out[size - channels :, :] = profile
        embed_out[...] = tn(profile_out[...], emb_ref[...]).astype(BF)


def encode_inner(image_rows, enc, channels):
    rows, lanes, frames = image_rows.shape
    map_rows = rows // 2
    width = enc.shape[0]
    line = GROUPS * width
    map_spec = pl.BlockSpec((1, line, frames), lambda i: (i + 1, 0, 0))
    map_shape = jax.ShapeDtypeStruct((map_rows, line, frames), BF)
    inner = map_rows - 2
    return pl.pallas_call(
        encode_inner_kernel,
        grid=(inner,),
        in_specs=[
            pl.BlockSpec((1, lanes, frames), lambda i: (2 * i + 3, 0, 0)),
            pl.BlockSpec((1, lanes, frames), lambda i: (2 * i + 4, 0, 0)),
            pl.BlockSpec((1, lanes, frames), lambda i: (1, 0, 0)),
            pl.BlockSpec((1, lanes, frames), lambda i: (2, 0, 0)),
            whole(enc.shape),
        ],
        out_specs=[map_spec, pl.BlockSpec((channels, frames), lambda i: (i, 0))],
        out_shape=[map_shape, jax.ShapeDtypeStruct((inner * channels, frames), BF)],
        scratch_shapes=[
            pltpu.VMEM((4, lanes + 2 * PAD, frames), BF),
            pltpu.VMEM((enc.shape[1], GROUPS * frames), BF),
            pltpu.VMEM((width, GROUPS * frames), F32),
            pltpu.VMEM((channels, frames), F32),
        ],
        compiler_params=params(60),
        cost_estimate=cost(2 * inner * frames * line * 256, 4 * inner * frames * line, inner * frames * line),
        name="encode_inner",
    )(image_rows, image_rows, image_rows, image_rows, enc)


def encode_edge(image_rows, up, down, enc, emb, inner, feat):
    rows, lanes, frames = image_rows.shape
    map_rows, line, _ = feat.shape
    width = enc.shape[0]
    channels = emb.shape[0] // map_rows
    model = emb.shape[1]
    end = map_rows - 1
    map_spec = pl.BlockSpec((1, line, frames), lambda i: (i * end, 0, 0))
    map_shape = jax.ShapeDtypeStruct(feat.shape, BF)
    profile = (map_rows * channels, frames)
    row_specs_here = [
        pl.BlockSpec((1, lanes, frames), lambda i, k=k: (i * (rows - 3) + k, 0, 0)) for k in range(3)
    ]
    return pl.pallas_call(
        encode_edge_kernel,
        grid=(2,),
        in_specs=row_specs_here
        + [halo_spec(up, 0), halo_spec(down, 0)]
        + [whole(x.shape) for x in (enc, emb, inner)]
        + [pl.BlockSpec(memory_space=pl.ANY)],
        out_specs=[map_spec, whole(profile), whole((frames, model))],
        out_shape=[
            map_shape,
            jax.ShapeDtypeStruct(profile, BF),
            jax.ShapeDtypeStruct((frames, model), BF),
        ],
        scratch_shapes=[
            pltpu.VMEM((4, lanes + 2 * PAD, frames), BF),
            pltpu.VMEM((enc.shape[1], GROUPS * frames), BF),
            pltpu.VMEM((width, GROUPS * frames), F32),
            pltpu.VMEM((channels, frames), F32),
        ],
        input_output_aliases={8: 0},
        compiler_params=params(60),
        cost_estimate=cost(4 * frames * line * 256, 8 * frames * line, 2 * frames * line),
        name="encode_edge",
    )(image_rows, image_rows, image_rows, up, down, enc, emb, inner, feat)


def normed(values):
    center = values - jnp.mean(values, axis=-1, keepdims=True)
    spread = jnp.mean(center * center, axis=-1, keepdims=True)
    inverse = lax.rsqrt(spread + 1e-05)
    return center * inverse, inverse


def stacked_heads(pair, lane):
    zero = jnp.zeros_like(pair)
    first = lane < 64
    return jnp.concatenate([jnp.where(first, pair, zero), jnp.where(first, zero, pair)], axis=0)


def fetch(sources, targets, sems):
    copies = [pltpu.make_async_copy(src, dst, sems.at[k]) for k, (src, dst) in enumerate(zip(sources, targets))]
    for copy in copies:
        copy.start()
    return copies


def send(source, target, sem):
    copy = pltpu.make_async_copy(source, target, sem)
    copy.start()
    return copy


def block_forward_kernel(
    slots, part_ref, more_ref, keys_ok_ref, ln1_ref, ln2_ref, film_scale_ref, qkv_in, out_in, up_in, down_in,
    film_shift_in, joined_out, attend_out, context_out, middle_out, active_out, slope_out, state_out, scale_out,
    shift_out, qkv_ref, out_ref, up_ref, down_ref, film_shift_ref, joined_ref, attend_ref, context_ref, middle_ref,
    active_ref, slope_ref, in_sems, out_sems,
):
    copies = fetch(
        (qkv_in, out_in, up_in, down_in, film_shift_in), (qkv_ref, out_ref, up_ref, down_ref, film_shift_ref), in_sems
    )
    embedded = part_ref[...].astype(F32) + more_ref[...].astype(F32)
    frames, model = embedded.shape
    unit, _ = normed(embedded)
    low = (unit * ln1_ref[...]).astype(BF)
    copies[0].wait()
    joined_ref[...] = nn(low, qkv_ref[...]).astype(BF)
    sent = [send(joined_ref, joined_out, out_sems.at[0])]
    size = 128
    row = lax.broadcasted_iota(jnp.int32, (size, size), 0)
    col = lax.broadcasted_iota(jnp.int32, (size, size), 1)
    inside = (row // slots == col // slots) & (col <= row)
    scaling = 1.0 / math.sqrt(model // HEADS)
    for b in range(frames // size):
        part = slice(b * size, (b + 1) * size)
        allowed = inside & (keys_ok_ref[:, part] > 0.5)
        for pair in range(HEADS // 2):
            lanes = pair * 128
            queries = joined_ref[part, lanes : lanes + 128]
            keys = stacked_heads(joined_ref[part, model + lanes : model + lanes + 128], col)
            values = stacked_heads(joined_ref[part, 2 * model + lanes : 2 * model + lanes + 128], col)
            scores = nt(queries, keys) * scaling
            halves = []
            for half in range(2):
                some = jnp.where(allowed, scores[:, half * size : (half + 1) * size], -1e30)
                weights = jnp.exp(some - jnp.max(some, axis=-1, keepdims=True))
                weights = weights / jnp.sum(weights, axis=-1, keepdims=True)
                halves.append(weights.astype(BF))
            weights = jnp.concatenate(halves, axis=1)
            attend_ref[b * HEADS // 2 + pair] = weights
            context_ref[part, lanes : lanes + 128] = nn(weights, values).astype(BF)
    sent.append(send(attend_ref, attend_out, out_sems.at[1]))
    sent.append(send(context_ref, context_out, out_sems.at[2]))
    copies[1].wait()
    middle = embedded + nn(context_ref[...], out_ref[...])
    middle_ref[...] = middle
    sent.append(send(middle_ref, middle_out, out_sems.at[3]))
    unit, _ = normed(middle)
    low = (unit * ln2_ref[...]).astype(BF)
    hidden = up_ref.shape[1]
    copies[2].wait()
    for start in range(0, hidden, 512):
        lanes = slice(start, start + 512)
        result, slope = gelu_pair(nn(low, up_ref[:, lanes]))
        active_ref[:, lanes] = result.astype(BF)
        slope_ref[:, lanes] = slope.astype(BF)
    sent.append(send(active_ref, active_out, out_sems.at[4]))
    sent.append(send(slope_ref, slope_out, out_sems.at[5]))
    copies[3].wait()
    state = (middle + nn(active_ref[...], down_ref[...])).astype(BF)
    state_out[...] = state
    scale_out[...] = nt(film_scale_ref[...], state) + 1.0
    copies[4].wait()
    shift_out[...] = tt(film_shift_ref[...], state)
    for copy in sent:
        copy.wait()


def block_forward(slots, parts, keys_ok, ln1, qkv, out_w, ln2, up_w, down_w, film_scale, film_shift):
    frames, model = parts[0].shape
    hidden = up_w.shape[1]
    blocks = frames // 128
    saved = [
        ((frames, 3 * model), BF),
        ((blocks * HEADS // 2, 128, 256), BF),
        ((frames, model), BF),
        ((frames, model), F32),
        ((frames, hidden), BF),
        ((frames, hidden), BF),
    ]
    shapes = [
        ((frames, model), BF),
        ((film_scale.shape[0], frames), F32),
        ((film_shift.shape[1], frames), F32),
    ]
    flops = 2 * frames * model * (3 * model + model + 2 * hidden)
    vmem, hbm = pl.BlockSpec(memory_space=pltpu.VMEM), pl.BlockSpec(memory_space=pl.ANY)
    staged = (qkv, out_w, up_w, down_w, film_shift)
    return pl.pallas_call(
        functools.partial(block_forward_kernel, slots),
        in_specs=[vmem] * 6 + [hbm] * len(staged),
        out_specs=[hbm] * len(saved) + [vmem] * len(shapes),
        out_shape=[jax.ShapeDtypeStruct(*s) for s in saved + shapes],
        scratch_shapes=[pltpu.VMEM(w.shape, w.dtype) for w in staged]
        + [pltpu.VMEM(*s) for s in saved]
        + [pltpu.SemaphoreType.DMA((len(staged),)), pltpu.SemaphoreType.DMA((len(saved),))],
        compiler_params=params(60),
        cost_estimate=cost(flops, 16 * 1024 * 1024, frames * hidden),
        name="block_forward",
    )(*parts, keys_ok, ln1, ln2, film_scale, *staged)


def decoded_grad_kernel(base, odd, a_ref, b_ref, c_ref, d_ref, one_ref, two_ref, down_ref, live_ref, dec_ref, *rest):
    out_ref, ring_scr, window_scr, grad_scr = rest[-4:]
    step = pl.program_id(0)
    _, lanes, frames = down_ref.shape
    width, depth = dec_ref.shape
    start = (lambda: one_ref[0], lambda: two_ref[0])
    fill_six(
        ring_scr, step == 0, step + base == odd, start, (a_ref, b_ref, c_ref, d_ref), down_ref, live_ref[...]
    )
    dec = dec_ref[...] * 0.5
    for r in range(2):
        fill_windows_at(window_scr, ring_scr, 2 * r, depth // SLOT, lanes // GROUPS)
        grad_scr[...] = nn(dec, window_scr[...])
        for g in range(GROUPS):
            for tile, column in tiles(frames, g):
                out_ref[r, g * width : (g + 1) * width, tile] = grad_scr[:, column].astype(BF)


def decoded_grad(recon_rows, up, down, live, dec_cols, base, steps, before):
    rows, lanes, frames = recon_rows.shape
    map_rows = rows // 2
    width, depth = dec_cols.shape
    line = GROUPS * width
    one = up if base == 0 else recon_rows
    row_shape = (1, lanes, frames)
    return pl.pallas_call(
        functools.partial(decoded_grad_kernel, base, map_rows // 2 - 1),
        grid=(steps,),
        in_specs=four_row_specs(frames, lanes, rows, base)
        + [
            halo_spec(up, 1) if base == 0 else pl.BlockSpec(row_shape, lambda i: (4 * base - 1, 0, 0)),
            pl.BlockSpec(row_shape, lambda i: (4 * base, 0, 0)),
            halo_spec(down, 1),
            whole(live.shape),
            whole(dec_cols.shape),
        ]
        + [pl.BlockSpec(memory_space=pl.ANY)] * len(before),
        out_specs=pl.BlockSpec((2, line, frames), lambda i: (i + base, 0, 0)),
        out_shape=jax.ShapeDtypeStruct((map_rows, line, frames), BF),
        scratch_shapes=[
            pltpu.VMEM((6, lanes + 2 * PAD, frames), BF),
            pltpu.VMEM((depth, GROUPS * frames), BF),
            pltpu.VMEM((width, GROUPS * frames), F32),
        ],
        input_output_aliases={9: 0} if before else {},
        compiler_params=params(60),
        cost_estimate=cost(4 * steps * frames * line * 256, 4 * steps * frames * line),
        name="decoded_grad",
    )(*[recon_rows] * 4, one, recon_rows, down, live, dec_cols, *before)


def decode_kernel(
    feat_ref, grad_ref, scale_ref, shift_ref, film_scale_ref, film_shift_ref,
    back_out, scale_grad_out, shift_grad_out, film_out, scale_scr, shift_grad_scr,
):
    step = pl.program_id(0)
    last = pl.num_programs(0) - 1
    channels, frames = scale_scr.shape
    line = feat_ref.shape[1]

    @pl.when(step == 0)
    def _():
        scale_scr[...] = jnp.zeros_like(scale_scr)

    scale = (scale_ref[...] * SHRINK).astype(BF)
    scaled = None
    for r in range(2):
        shift = (shift_ref[r * channels : (r + 1) * channels, :] * SHRINK).astype(BF)
        total = None
        for g in range(0, line, 4 * channels):
            backs, terms = [], []
            for j in range(g, g + 4 * channels, channels):
                rows = slice(j, j + channels)
                feat = feat_ref[r, rows, :]
                back = grad_ref[r, rows, :] * double_slope(feat * scale + shift)
                back_out[r, rows, :] = back
                backs.append(back)
                terms.append(back * feat)
            total = wide_sum(backs) if total is None else total + wide_sum(backs)
            scaled = wide_sum(terms) if scaled is None else scaled + wide_sum(terms)
        shift_grad_scr[2 * step + r] = total.astype(BF)
    scale_scr[...] += scaled

    @pl.when(step == last)
    def _():
        scale_grad = scale_scr[...].astype(BF)
        shift_grad = shift_grad_scr[...].reshape(shift_grad_out.shape)
        scale_grad_out[...] = scale_grad
        shift_grad_out[...] = shift_grad
        film_out[...] = (tn(scale_grad, film_scale_ref[...]) + tt(shift_grad, film_shift_ref[...])).astype(BF)


def decode(feat, grad, scale, shift, film_scale, film_shift):
    map_rows, line, frames = feat.shape
    channels, model = film_scale.shape
    map_spec = pl.BlockSpec((2, line, frames), lambda i: (i, 0, 0))
    grads = [
        jax.ShapeDtypeStruct((channels, frames), BF),
        jax.ShapeDtypeStruct((map_rows * channels, frames), BF),
        jax.ShapeDtypeStruct((frames, model), BF),
    ]
    return pl.pallas_call(
        decode_kernel,
        grid=(map_rows // 2,),
        in_specs=[
            map_spec,
            map_spec,
            whole(scale.shape),
            pl.BlockSpec((2 * channels, frames), lambda i: (i, 0)),
            whole(film_scale.shape),
            whole(film_shift.shape),
        ],
        out_specs=[map_spec] + [whole(g.shape) for g in grads],
        out_shape=[jax.ShapeDtypeStruct((map_rows, line, frames), BF)] + grads,
        scratch_shapes=[
            pltpu.VMEM((channels, frames), F32),
            pltpu.VMEM((map_rows, channels, frames), BF),
        ],
        compiler_params=params(60),
        cost_estimate=cost(20 * map_rows * frames * line, 6 * map_rows * frames * line, map_rows * frames * line),
        name="decode",
    )(feat, grad, scale, shift, film_scale, film_shift)


def blocks_to_lanes(values, rows):
    return jnp.concatenate([values[s : s + rows] for s in range(0, values.shape[0], rows)], axis=1)


def put(own_ref, other_ref, core, start, values):
    size, lanes = own_ref.shape[0], slice(start, start + values.shape[1])
    low = values.astype(BF)
    first = core == 0
    own_ref[:, lanes] = jnp.where(first, low[:size], low[size:])
    other_ref[:, lanes] = jnp.where(first, low[size:], low[:size])


def heads_kernel(
    place_ref, state_ref, cot_ref, live_ref, prior_ref, scale_grad_ref, shift_grad_ref, own_out, other_out,
    stream_out,
):
    live = live_ref[:, :1]
    grad = (cot_ref[...].astype(F32) * live).astype(BF)
    size = 2 * own_out.shape[0]
    core = place_ref[1]
    logits = grad.shape[1]
    state = state_ref[...]
    model = state.shape[1]
    start = pl.multiple_of(place_ref[0] * size, size)
    put(own_out, other_out, core, 0, tn(state_ref[:, pl.ds(start, size)], grad))
    stream_out[...] = nt(grad, prior_ref[...])
    scale_grad = nn(scale_grad_ref[...], state)
    blank = jnp.zeros((size - scale_grad.shape[0], model), F32)
    put(own_out, other_out, core, logits, jnp.concatenate([scale_grad, blank], axis=0))
    put(own_out, other_out, core, logits + model, blocks_to_lanes(nn(shift_grad_ref[...], state), size))


def heads(place, parts, state, logit_cot, live_cols, prior_w, scale_grad, shift_grad):
    frames, model = state.shape
    logits = logit_cot.shape[1]
    size = model // parts
    width = logits + model + shift_grad.shape[0] // size * model
    vmem = pl.BlockSpec(memory_space=pltpu.VMEM)
    return pl.pallas_call(
        heads_kernel,
        in_specs=[pl.BlockSpec(memory_space=pltpu.SMEM)] + [vmem] * 6,
        out_shape=[jax.ShapeDtypeStruct((size // 2, width), BF)] * 2
        + [jax.ShapeDtypeStruct((frames, model), F32)],
        compiler_params=params(60),
        cost_estimate=cost(4 * frames * model * logits, 4 * 1024 * 1024),
        name="heads",
    )(place, state, logit_cot, live_cols, prior_w, scale_grad, shift_grad)


def norm_backward(grad, unit, inverse):
    return (
        grad
        - jnp.mean(grad, axis=-1, keepdims=True)
        - unit * jnp.mean(grad * unit, axis=-1, keepdims=True)
    ) * inverse


def block_backward_kernel(
    columns, place_ref, part_ref, more_ref, embed_part_ref, embed_more_ref, stream_ref, ln1_ref, ln2_ref,
    down_in, slope_in, active_in, middle_in, up_in, context_in, out_in, joined_in, attend_in, qkv_in, emb_in,
    profile_in, own_out, other_out, profile_out, down_ref, slope_ref, active_ref, middle_ref, up_ref, context_ref, out_ref,
    joined_ref, attend_ref, qkv_ref, emb_ref, profile_ref, raised_scr, low_scr, grad_scr, in_sems,
):
    names = ("down", "slope", "active", "middle", "up", "context", "out", "joined", "attend", "qkv", "emb", "profile")
    sources = (
        down_in, slope_in, active_in, middle_in, up_in, context_in, out_in, joined_in, attend_in, qkv_in, emb_in,
        profile_in,
    )
    targets = (
        down_ref, slope_ref, active_ref, middle_ref, up_ref, context_ref, out_ref, joined_ref, attend_ref, qkv_ref,
        emb_ref, profile_ref,
    )
    copies = dict(zip(names, fetch(sources, targets, in_sems)))
    grad_out = stream_ref[...] + part_ref[...].astype(F32) + more_ref[...].astype(F32)
    frames, model = grad_out.shape
    hidden = up_ref.shape[1]
    branch = grad_out.astype(BF)
    place, core = place_ref[0], place_ref[1]
    size = 2 * own_out.shape[0]
    start_qkv, start_out, start_down = hidden, hidden + 3 * model, hidden + 4 * model
    start_norm = start_down + hidden // model * model
    copies["down"].wait()
    copies["slope"].wait()
    for start in range(0, hidden, 512):
        lanes = slice(start, start + 512)
        raised_scr[:, lanes] = (nt(branch, down_ref[lanes, :]) * slope_ref[:, lanes].astype(F32)).astype(BF)
    copies["active"].wait()
    for s in range(0, hidden, model):
        some = active_ref[:, pl.ds(pl.multiple_of(place * size + s, size), size)]
        put(own_out, other_out, core, start_down + s, tn(some, branch))
    copies["middle"].wait()
    middle = middle_ref[...]
    unit, inverse = normed(middle)
    low_scr[...] = (unit * ln2_ref[...]).astype(BF)
    window = pl.ds(pl.multiple_of(place * size, size), size)
    put(own_out, other_out, core, 0, tn(low_scr[:, window], raised_scr[...]))
    copies["up"].wait()
    grad = nt(raised_scr[...], up_ref[...])
    norm_two = jnp.sum(grad * unit, axis=0, keepdims=True)
    grad_middle = grad_out + norm_backward(grad * ln2_ref[...], unit, inverse)
    attended = grad_middle.astype(BF)
    copies["context"].wait()
    put(own_out, other_out, core, start_out, tn(context_ref[:, window], attended))
    copies["out"].wait()
    low_scr[...] = nt(attended, out_ref[...]).astype(BF)
    block = 128
    col = lax.broadcasted_iota(jnp.int32, (block, block), 1)
    first = col < 64
    scaling = 1.0 / math.sqrt(model // HEADS)
    copies["joined"].wait()
    copies["attend"].wait()
    for b in range(frames // block):
        part = slice(b * block, (b + 1) * block)
        for pair in range(HEADS // 2):
            lanes = pair * 128
            queries = joined_ref[part, lanes : lanes + 128]
            keys = stacked_heads(joined_ref[part, model + lanes : model + lanes + 128], col)
            values = stacked_heads(joined_ref[part, 2 * model + lanes : 2 * model + lanes + 128], col)
            grads = low_scr[part, lanes : lanes + 128]
            weights_low = attend_ref[b * HEADS // 2 + pair]
            weights = weights_low.astype(F32)
            terms = weights * nt(grads, values)
            halves = []
            for half in range(2):
                some = slice(half * block, (half + 1) * block)
                inner = jnp.sum(terms[:, some], axis=-1, keepdims=True)
                halves.append((terms[:, some] - weights[:, some] * inner).astype(BF))
            grad_scores = jnp.concatenate(halves, axis=1)
            grad_queries = nn(grad_scores, keys)
            both = tn(grad_scores, queries)
            grad_keys = jnp.where(first, both[:block], both[block:])
            both = tn(weights_low, grads)
            grad_values = jnp.where(first, both[:block], both[block:])
            for k, term in enumerate((grad_queries * scaling, grad_keys * scaling, grad_values)):
                grad_scr[part, k * model + lanes : k * model + lanes + 128] = term.astype(BF)
    unit, inverse = normed(embed_part_ref[...].astype(F32) + embed_more_ref[...].astype(F32))
    low_scr[...] = (unit * ln1_ref[...]).astype(BF)
    put(own_out, other_out, core, start_qkv, tn(low_scr[:, window], grad_scr[...]))
    copies["qkv"].wait()
    grad = nt(grad_scr[...], qkv_ref[...])
    norm_one = jnp.sum(grad * unit, axis=0, keepdims=True)
    lines = [norm[:, s : s + 128] for norm in (norm_one, norm_two) for s in range(0, model, 128)]
    lines.append(jnp.zeros((size - len(lines), 128), F32))
    put(own_out, other_out, core, start_norm, jnp.concatenate(lines, axis=0))
    grad_embed = (grad_middle + norm_backward(grad * ln1_ref[...], unit, inverse)).astype(BF)
    copies["emb"].wait()
    profile_out[...] = nt(emb_ref[...], grad_embed) * (1.0 / columns)
    copies["profile"].wait()
    put(own_out, other_out, core, start_norm + 128, blocks_to_lanes(nn(profile_ref[...], grad_embed), size))


def block_backward(
    columns, parts, place, grads, embeds, stream, joined, attend, context, middle, active, slope, profile,
    ln1, qkv, out_w, ln2, up_w, down_w, emb,
):
    frames, model = stream.shape
    hidden = up_w.shape[1]
    size = model // parts
    width = 2 * hidden + 4 * model + 128 + emb.shape[0] // size * model
    shapes = [((size // 2, width), BF), ((size // 2, width), BF), (profile.shape, F32)]
    vmem, hbm = pl.BlockSpec(memory_space=pltpu.VMEM), pl.BlockSpec(memory_space=pl.ANY)
    near = (*grads, *embeds, stream, ln1, ln2)
    staged = (down_w, slope, active, middle, up_w, context, out_w, joined, attend, qkv, emb, profile)
    return pl.pallas_call(
        functools.partial(block_backward_kernel, columns),
        in_specs=[pl.BlockSpec(memory_space=pltpu.SMEM)] + [vmem] * len(near) + [hbm] * len(staged),
        out_shape=[jax.ShapeDtypeStruct(*s) for s in shapes],
        scratch_shapes=[pltpu.VMEM(x.shape, x.dtype) for x in staged]
        + [
            pltpu.VMEM((frames, hidden), BF),
            pltpu.VMEM((frames, model), BF),
            pltpu.VMEM((frames, 3 * model), BF),
            pltpu.SemaphoreType.DMA((len(staged),)),
        ],
        compiler_params=params(60),
        cost_estimate=cost(3 * frames * model * (4 * model + 2 * hidden), 20 * 1024 * 1024),
        name="block_backward",
    )(place, *near, *staged)


def scatter_body(
    step, last, row_refs, first_ref, up_ref, down_ref, live, matrix_ref, places_ref, outs, scrs, fill
):
    rows_out, rim_up_out, rim_down_out, taps_out = outs
    ring_scr, window_scr, low_scr, rows_scr, held_scr, cov_scr = scrs
    _, lanes, frames = up_ref.shape
    depth, _ = matrix_ref.shape
    stride = lanes // GROUPS
    inner = slice(PAD, PAD + lanes)
    kind = rows_out.dtype

    @pl.when(step == 0)
    def _():
        cov_scr[...] = jnp.zeros_like(cov_scr)
        rows_scr[...] = jnp.zeros_like(rows_scr)
        held_scr[...] = jnp.zeros_like(held_scr)

    rows_out[0:3] = held_scr[...]

    @pl.when(step < last)
    def _():
        fill_six(
            ring_scr, step == 0, step == last - 1, (lambda: up_ref[0], lambda: first_ref[0]), row_refs, down_ref,
            live,
        )
        matrix = matrix_ref[...]
        for r in range(2):
            fill_windows_at(window_scr, ring_scr, 2 * r, depth // SLOT, stride)
            fill(r)
            placed = nn(matrix, low_scr[...])
            for g in range(GROUPS):
                add_rows(rows_scr, 2 * r, placed[:, g * frames : (g + 1) * frames], g, stride)
            cov_scr[...] += nt(low_scr[...], window_scr[...])

    rows_out[3] = rows_scr[0, inner, :].astype(kind)

    @pl.when(step == 0)
    def _():
        rim_up_out[...] = rows_scr[0, inner, :].astype(BF)

    @pl.when(step == last)
    def _():
        rim_down_out[...] = rows_scr[1, inner, :].astype(BF)
        taps_out[...] = fold_taps(cov_scr, places_ref, taps_out.shape[1])

    @pl.when(step < last)
    def _():
        held_scr[...] = rows_scr[1:4, inner, :].astype(kind)
        rows_scr[0:2] = rows_scr[4:6]
        rows_scr[2:6] = jnp.zeros((4,) + rows_scr.shape[1:], F32)


def rebuild_kernel(
    feat_ref, a_ref, b_ref, c_ref, d_ref, first_ref, up_ref, down_ref, live_ref, dec_ref, scale_ref, shift_ref,
    places_ref, rows_out, rim_up_out, rim_down_out, taps_out,
    ring_scr, window_scr, low_scr, rows_scr, held_scr, cov_scr,
):
    frames = up_ref.shape[2]
    width = dec_ref.shape[1]
    channels = scale_ref.shape[0]

    def fill(r):
        scale = (scale_ref[...] * 0.5).astype(BF)
        shift = (shift_ref[r * channels : (r + 1) * channels, :] * 0.5).astype(BF)
        for g in range(GROUPS):
            for tile, column in tiles(frames, g):
                for j in range(0, width, channels):
                    feat = feat_ref[r, g * width + j : g * width + j + channels, tile]
                    low_scr[j : j + channels, column] = gelu_of_half(feat * scale[:, tile] + shift[:, tile])

    scatter_body(
        pl.program_id(0), pl.num_programs(0) - 1, (a_ref, b_ref, c_ref, d_ref), first_ref, up_ref, down_ref,
        live_ref[...], dec_ref, places_ref, (rows_out, rim_up_out, rim_down_out, taps_out),
        (ring_scr, window_scr, low_scr, rows_scr, held_scr, cov_scr), fill,
    )


def encode_backward_kernel(
    back_ref, a_ref, b_ref, c_ref, d_ref, first_ref, up_ref, down_ref, enc_cols_ref, enc_ref, scale_ref, profile_ref,
    places_ref, rows_out, rim_up_out, rim_down_out, taps_out,
    ring_scr, window_scr, low_scr, rows_scr, held_scr, cov_scr, value_scr,
):
    frames = up_ref.shape[2]
    width = enc_ref.shape[1]
    channels = scale_ref.shape[0]

    def fill(r):
        value_scr[...] = nn(enc_cols_ref[...], window_scr[...])
        scale = (scale_ref[...] * 0.5).astype(BF)
        mean = (profile_ref[r * channels : (r + 1) * channels, :] * 0.5).astype(BF)
        for g in range(GROUPS):
            for tile, column in tiles(frames, g):
                for j in range(0, width, channels):
                    back = back_ref[r, g * width + j : g * width + j + channels, tile]
                    slope = double_slope((value_scr[j : j + channels, column] * SHRINK).astype(BF))
                    low_scr[j : j + channels, column] = (back * scale[:, tile] + mean[:, tile]) * slope

    scatter_body(
        pl.program_id(0), pl.num_programs(0) - 1, (a_ref, b_ref, c_ref, d_ref), first_ref, up_ref, down_ref,
        None, enc_ref, places_ref, (rows_out, rim_up_out, rim_down_out, taps_out),
        (ring_scr, window_scr, low_scr, rows_scr, held_scr, cov_scr), fill,
    )


def scatter_call(kernel, name, kind, which, map_in, rows_in, up, down, more, more_specs, width, depth, channels):
    rows, lanes, frames = rows_in.shape
    steps = rows // 4
    line = GROUPS * width
    rim = jax.ShapeDtypeStruct((lanes, frames), BF)
    taps = jax.ShapeDtypeStruct((more[-1].shape[1], channels), F32)
    scratch = [
        pltpu.VMEM((6, lanes + 2 * PAD, frames), BF),
        pltpu.VMEM((depth, GROUPS * frames), BF),
        pltpu.VMEM((width, GROUPS * frames), BF),
        pltpu.VMEM((6, lanes + 2 * PAD, frames), F32),
        pltpu.VMEM((3, lanes, frames), kind),
        pltpu.VMEM((width, depth), F32),
    ]
    if which == 0:
        scratch.append(pltpu.VMEM((width, GROUPS * frames), F32))
    return pl.pallas_call(
        kernel,
        grid=(steps + 1,),
        in_specs=[pl.BlockSpec((2, line, frames), lambda i: (jnp.minimum(i, steps - 1), 0, 0))]
        + four_row_specs(frames, lanes, rows)
        + [pl.BlockSpec((1, lanes, frames), lambda i: (0, 0, 0)), halo_spec(up, which), halo_spec(down, which)]
        + more_specs,
        out_specs=[
            pl.BlockSpec((4, lanes, frames), lambda i: (jnp.maximum(i - 1, 0), 0, 0)),
            whole(rim.shape),
            whole(rim.shape),
            whole(taps.shape),
        ],
        out_shape=[jax.ShapeDtypeStruct((rows, lanes, frames), kind), rim, rim, taps],
        scratch_shapes=scratch,
        compiler_params=params(60),
        cost_estimate=cost(4 * rows * frames * line * 128, 2 * rows * frames * line),
        name=name,
    )(map_in, *[rows_in] * 5, up, down, *more)


def row_block(channels, frames, rows):
    return pl.BlockSpec((2 * channels, frames), lambda i: (jnp.minimum(i, rows // 4 - 1), 0))


def rebuild(feat, recon_rows, up, down, live, dec, scale, shift, places):
    rows, _, frames = recon_rows.shape
    channels = scale.shape[0]
    return scatter_call(
        rebuild_kernel, "rebuild", BF, 1, feat, recon_rows, up, down, (live, dec, scale, shift, places),
        [whole(live.shape), whole(dec.shape), whole(scale.shape), row_block(channels, frames, rows), whole(places.shape)],
        dec.shape[1], dec.shape[0], channels,
    )


def encode_backward(back, image_rows, up, down, enc_cols, enc, scale, profile, places):
    rows, _, frames = image_rows.shape
    channels = scale.shape[0]
    return scatter_call(
        encode_backward_kernel, "encode_backward", F32, 0, back, image_rows, up, down,
        (enc_cols, enc, scale, profile, places),
        [
            whole(enc_cols.shape), whole(enc.shape), whole(scale.shape), row_block(channels, frames, rows),
            whole(places.shape),
        ],
        enc.shape[1], enc.shape[0], channels,
    )


def rims_kernel(low_ref, wide_ref, above_ref, below_ref, low_out, wide_out):
    for at, rim_ref in ((0, above_ref), (1, below_ref)):

        @pl.when(pl.program_id(0) == at)
        def _(rim_ref=rim_ref):
            for k, (rows_ref, out_ref) in enumerate(((low_ref, low_out), (wide_ref, wide_out))):
                out_ref[0] = (rows_ref[0].astype(F32) + rim_ref[k].astype(F32)).astype(out_ref.dtype)


def with_rims(low, wide, above, below):
    count, lanes, frames = low.shape
    row_spec = pl.BlockSpec((1, lanes, frames), lambda i: (i * (count - 1), 0, 0))
    return pl.pallas_call(
        rims_kernel,
        grid=(2,),
        in_specs=[row_spec, row_spec, whole(above.shape), whole(below.shape)],
        out_specs=[row_spec, row_spec],
        out_shape=[jax.ShapeDtypeStruct(low.shape, low.dtype), jax.ShapeDtypeStruct(wide.shape, wide.dtype)],
        input_output_aliases={0: 0, 1: 1},
        compiler_params=params(60),
        cost_estimate=cost(0, 16 * lanes * frames),
        name="with_rims",
    )(low, wide, above, below)


def send_along(values, axis, step):
    count = lax.axis_size(axis)
    pairs = [(i, i + step) for i in range(count) if 0 <= i + step < count]
    return lax.ppermute(values, axis, pairs)


def swap(values, axis, distance):
    count = lax.axis_size(axis)
    return lax.ppermute(values, axis, [(i, i ^ distance) for i in range(count)])


def cross(values, turn):
    rows, frames = lax.axis_size("rows"), lax.axis_size("frames")
    pairs = []
    for r in range(rows):
        for f in range(frames):
            distance = 1 + (f + turn) % 2
            pairs.append((r * frames + f, (r ^ distance) * frames + f))
    return lax.ppermute(values, ("rows", "frames"), pairs)


def add(values, more):
    return (values.astype(F32) + more.astype(F32)).astype(BF)


def chip_groups():
    count = lax.axis_size("frames")
    return [list(range(core, count, 2)) for core in range(2)]


def split_over(values, groups):
    count = len(groups[0])
    split = values.reshape((count, values.shape[0] // count) + values.shape[1:])
    return lax.all_to_all(split, "frames", 0, 0, axis_index_groups=groups)


def sum_parts(parts):
    return jnp.sum(parts.astype(F32), axis=0).astype(BF)


def gather_over(values, axis):
    count = lax.axis_size(axis)
    copies = jnp.broadcast_to(values[None], (count,) + values.shape)
    return lax.all_to_all(copies, axis, 0, 0)


def swap_frames(values, distance):
    count = lax.axis_size("frames")
    return lax.ppermute(values, "frames", [(f, f ^ distance) for f in range(count)])


def gather_chips(values):
    count = lax.axis_size("frames") // 2
    copies = jnp.broadcast_to(values[None], (count,) + values.shape)
    return lax.all_to_all(copies, "frames", 0, 0, axis_index_groups=chip_groups())


def finish_kernel(slots, widths, place_ref, *refs):
    count = len(slots)
    own_in, other_in = refs[:count], refs[count : 2 * count]
    outs, (own_scr, other_scr, sems) = refs[-10:-3], refs[-3:]
    scale_before = refs[-11]
    step = pl.program_id(0)
    core = place_ref[4]
    chips = own_scr.shape[1]
    copies = [
        [pltpu.make_async_copy(ref, scr.at[k], sems.at[side, k]) for k, ref in enumerate(sources)]
        for side, (sources, scr) in enumerate(((own_in, own_scr), (other_in, other_scr)))
    ]

    @pl.when(step == 0)
    def _():
        for k in range(count):
            copies[0][k].start()
            copies[1][k].start()

    for k in range(count):

        @pl.when(step == k)
        def _(k=k):
            copies[0][k].wait()
            copies[1][k].wait()
            for scr, half in ((own_scr, core), (other_scr, 1 - core)):
                for chip in range(chips):
                    at, piece = 0, half * chips + chip
                    for out, (kind, lanes) in zip(outs, widths):
                        part = scr[k, chip, :, at : at + lanes].astype(F32)
                        at += lanes
                        if kind == "row":
                            out[piece] = part
                        elif kind == "blocks":
                            size = out.shape[-1]
                            for block in range(out.shape[0]):
                                out[block, piece] = part[:, block * size : (block + 1) * size]
                        elif kind == "norm" and k == 0:
                            out[piece] = part
                        elif kind == "scale":
                            if k:
                                out[piece] += part
                            else:
                                out[piece] = part + scale_before[piece] if slots[0] else part


def finish(place, slots, own, other, before, logits, model, hidden):
    chips, size, lanes = own[0].shape
    pieces = 2 * chips
    quarters = 4
    many = hidden // model
    widths = (
        ("row", logits), ("scale", model), ("row", hidden), ("row", 3 * model), ("row", model), ("blocks", hidden),
        ("norm", 128),
    )
    specs, shapes = [], []
    for kind, width in widths:
        if kind == "blocks":
            shape, index = (many, pieces, size, model), lambda k, place: (0, place[slots[0] + k], 0, 0)
            shapes.append((many, quarters * pieces, size, model))
        elif kind == "row":
            shape, index = (pieces, size, width), lambda k, place: (place[slots[0] + k], 0, 0)
            shapes.append((quarters * pieces, size, width))
        else:
            shape, index = (pieces, size, width), lambda k, place: (0, 0, 0)
            shapes.append(shape)
        specs.append(pl.BlockSpec(shape, index))
    held = pltpu.VMEM((len(slots), chips, size, lanes), BF)
    arrays = len(own) + len(other)
    kept = [k for k, (kind, _) in enumerate(widths) if kind in ("row", "blocks")]
    more = [before[k] for k in kept] + [before[1]] if before else [jnp.zeros((1, 8, 128), F32)]
    return pl.pallas_call(
        functools.partial(finish_kernel, slots, widths),
        grid_spec=pltpu.PrefetchScalarGridSpec(
            num_scalar_prefetch=1,
            grid=(len(slots),),
            in_specs=[pl.BlockSpec(memory_space=pl.ANY)] * (arrays + len(more) - 1) + [whole(more[-1].shape)],
            out_specs=specs,
            scratch_shapes=[held, held, pltpu.SemaphoreType.DMA((2, len(slots)))],
        ),
        out_shape=[jax.ShapeDtypeStruct(shape, F32) for shape in shapes],
        input_output_aliases={1 + arrays + n: k for n, k in enumerate(kept)} if before else {},
        compiler_params=params(60),
        cost_estimate=cost(0, 10 * len(slots) * own[0].size),
        name="finish",
    )(place, *own, *other, *more)


def split_finish_kernel(place_ref, split_ref, split_other_ref, *outs):
    core = place_ref[4]
    chips = split_ref.shape[0]
    pieces = 2 * chips
    for ref, half in ((split_ref, core), (split_other_ref, 1 - core)):
        for chip in range(chips):
            at = 0
            for out in outs:
                lanes = out.shape[-1]
                for block in range(out.shape[0] // pieces):
                    out[block * pieces + half * chips + chip] = ref[chip, :, at : at + lanes].astype(F32)
                    at += lanes


def split_finish(place, split, split_other, model):
    chips, size, lanes = split.shape
    shape = (lanes // (2 * model) * 2 * chips, size, model)
    vmem = pl.BlockSpec(memory_space=pltpu.VMEM)
    return pl.pallas_call(
        split_finish_kernel,
        in_specs=[pl.BlockSpec(memory_space=pltpu.SMEM), vmem, vmem],
        out_shape=[jax.ShapeDtypeStruct(shape, F32)] * 2,
        compiler_params=params(40),
        cost_estimate=cost(0, 8 * split.size),
        name="split_finish",
    )(place, split, split_other)


def on_device(
    images, enc_kernel, emb_weight, ln1_gain, qkv_weight, out_weight, ln2_gain, up_weight, down_weight,
    prior_weight, film_scale, film_shift, dec_kernel, horizons, frame_valid, recon_cot, logit_cot,
):
    frames, rows, lanes = images.shape
    taps, _, chan_in, channels = enc_kernel.shape
    columns = lanes // chan_in // 2
    copies = columns // GROUPS
    model = qkv_weight.shape[0]
    hidden = up_weight.shape[1]
    slots = frames // horizons.shape[0]
    count = lax.axis_size("rows")

    places = jnp.asarray(tap_places(taps, chan_in, copies), BF)
    enc_taps = jnp.transpose(enc_kernel, (0, 2, 1, 3)).reshape(taps * chan_in * taps, channels)
    dec_taps = jnp.transpose(dec_kernel, (0, 3, 1, 2)).reshape(taps * chan_in * taps, channels)
    film_scale_rows = film_scale.T
    image_rows = jnp.transpose(images, (1, 2, 0))
    recon_rows = jnp.transpose(recon_cot, (1, 2, 0))

    steps = jnp.arange(slots)
    reached = (steps[None, :] <= horizons[:, None]).reshape(frames)
    live = (reached & (frame_valid > 0)).astype(F32)
    live_cols = jnp.broadcast_to(live[:, None], (frames, 128))
    keys_ok = reached.astype(F32)[None, :]
    place = jnp.stack([lax.axis_index("rows"), lax.axis_index("frames") % 2]).astype(jnp.int32)

    above = send_along(jnp.stack([image_rows[-1], recon_rows[-1]]), "rows", 1)
    below = send_along(jnp.stack([image_rows[0], recon_rows[0]]), "rows", -1)
    enc_cols, enc, dec_cols, dec = expand(enc_taps, dec_taps, places)

    feat, inner = encode_inner(image_rows, enc_cols, channels)
    feat, profile, embed_part = encode_edge(image_rows, above, below, enc_cols, emb_weight, inner, feat)
    recon_later, embed_part = lax.optimization_barrier((recon_rows, embed_part))
    embed_more = cross(embed_part, 0)
    half = rows // 8
    decoded_args = (recon_later, above, below, live[None, :], dec_cols)
    grad = decoded_grad(*decoded_args, 0, half, ())
    embed_more, grad = lax.optimization_barrier((embed_more, grad))
    embed_part = add(embed_part, embed_more)
    embed_more = cross(embed_part, 1)
    grad = decoded_grad(*decoded_args, half, rows // 4 - half, (grad,))
    embed_more, grad = lax.optimization_barrier((embed_more, grad))
    embeds = embed_part, embed_more
    joined, attend, context, middle, active, active_slope, state, scale, shift = block_forward(
        slots, embeds, keys_ok, ln1_gain[None], qkv_weight, out_weight, ln2_gain[None], up_weight, down_weight,
        film_scale_rows, film_shift,
    )
    back, scale_grad, shift_grad, film_part = decode(feat, grad, scale, shift, film_scale_rows, film_shift)
    film_more = cross(film_part, 0)
    head_own, head_other, stream = heads(place, count, state, logit_cot, live_cols, prior_weight, scale_grad, shift_grad)
    film_more, head_other = lax.optimization_barrier((film_more, head_other))
    film_part = add(film_part, film_more)
    film_more = cross(film_part, 1)
    head_half_sum = add(head_own, swap_frames(head_other, 1))
    head_parts = split_over(head_half_sum, chip_groups())
    block_own, block_other, grad_profile = block_backward(
        columns, count, place, (film_part, film_more), embeds, stream, joined, attend, context, middle, active,
        active_slope, profile, ln1_gain[None], qkv_weight, out_weight, ln2_gain[None], up_weight, down_weight,
        emb_weight,
    )
    head_parts, block_other = lax.optimization_barrier((head_parts, block_other))
    head_piece = sum_parts(head_parts)
    logits = prior_weight.shape[1]
    head_lanes, block_lanes = logits + model, 2 * hidden + 4 * model + 128
    block_more = swap_frames(block_other, 1)
    block_half_sum = add(block_own, block_more)
    feat, block_half_sum = lax.optimization_barrier((feat, block_half_sum))
    block_parts = split_over(block_half_sum, chip_groups())
    rebuilt_rows, rim_up, rim_down, dec_cov = rebuild(
        feat, recon_rows, above, below, live[None, :], dec, scale, shift, places
    )
    block_parts, dec_cov = lax.optimization_barrier((block_parts, dec_cov))
    block_piece = sum_parts(block_parts)
    shared = jnp.concatenate([head_piece[:, :head_lanes], block_piece[:, :block_lanes]], axis=1)
    shared, back = lax.optimization_barrier((shared, back))
    own = gather_chips(shared)
    image_grad, image_up, image_down, enc_cov = encode_backward(
        back, image_rows, above, below, enc_cols, enc, scale, grad_profile, places
    )
    own, enc_cov = lax.optimization_barrier((own, enc_cov))
    near, far, own_other = cross(own, 0), cross(own, 1), swap_frames(own, 1)
    covs = jnp.concatenate([enc_cov, dec_cov], axis=1)
    step = lax.axis_size("frames") // 2
    while step:
        covs = covs + swap_frames(covs, step)
        step //= 2
    row, core = lax.axis_index("rows"), lax.axis_index("frames") % 2
    slots_of = jnp.stack([row, row ^ (1 + core), row ^ (2 - core), row ^ 3, core]).astype(jnp.int32)
    split = gather_chips(jnp.concatenate([head_piece[:, head_lanes:], block_piece[:, block_lanes:]], axis=1))
    near, far, own_other, covs, split = lax.optimization_barrier((near, far, own_other, covs, split))
    both = cross(near, 1)
    near_other, far_other = swap_frames(near, 1), swap_frames(far, 1)
    found = finish(
        slots_of, (0, 1, 2), (own, near, far), (own_other, far_other, near_other), (), logits, model, hidden
    )
    film_shift_grad, emb_grad = split_finish(slots_of, split, swap_frames(split, 1), model)
    film_shift_grad = film_shift_grad.reshape(-1, model).T
    emb_grad = emb_grad.reshape(-1, model)
    norm_grads = found[6].reshape(-1, 128)[: 2 * model // 128].reshape(2, model)
    rims = jnp.stack([rim_down, image_down]), jnp.stack([rim_up, image_up])
    both, covs, rims, film_shift_grad, emb_grad, norm_grads, *found = lax.optimization_barrier(
        (both, covs, rims, film_shift_grad, emb_grad, norm_grads, *found)
    )
    both_other = swap_frames(both, 1)
    rims_above, rims_below = send_along(rims[0], "rows", 1), send_along(rims[1], "rows", -1)
    one, two, three = [lax.ppermute(covs, "rows", [(r, r ^ d) for r in range(count)]) for d in (1, 2, 3)]
    covs = (covs + one) + (two + three)
    found = finish(slots_of, (3,), (both,), (both_other,), found, logits, model, hidden)
    prior_grad, misc, up_grad, qkv_grad, out_grad, down_grad = [
        array.reshape(-1, array.shape[-1]) for array in found[:6]
    ]
    film_scale_grad = misc[:channels].T
    rims_above, rims_below, film_scale_grad, prior_grad = lax.optimization_barrier(
        (rims_above, rims_below, film_scale_grad, prior_grad)
    )
    rebuilt_rows, image_grad = with_rims(rebuilt_rows, image_grad, rims_above, rims_below)
    enc_cov, dec_cov = covs[:, :channels], covs[:, channels:]
    enc_grad = jnp.transpose(enc_cov.reshape(taps, chan_in, taps, channels), (0, 2, 1, 3))
    dec_grad = jnp.transpose(dec_cov.reshape(taps, chan_in, taps, channels), (0, 2, 3, 1))
    return (
        jnp.transpose(rebuilt_rows, (2, 0, 1)),
        jnp.transpose(image_grad, (2, 0, 1)),
        enc_grad,
        emb_grad,
        norm_grads[0],
        qkv_grad,
        out_grad,
        norm_grads[1],
        up_grad,
        down_grad,
        prior_grad,
        film_scale_grad,
        film_shift_grad,
        dec_grad,
    )


def solution(mesh):
    return jax.shard_map(
        on_device,
        mesh=mesh,
        in_specs=(
            P("frames", "rows", None),
            P(),
            P("rows", None),
            P(),
            P(),
            P(),
            P(),
            P(),
            P(),
            P(),
            P(),
            P(None, "rows"),
            P(),
            P("frames"),
            P("frames"),
            P("frames", "rows", None),
            P("frames", None),
        ),
        out_specs=(
            P("frames", "rows", None),
            P("frames", "rows", None),
            P(),
            P("rows", None),
            P(),
            P(),
            P(),
            P(),
            P(),
            P(),
            P(),
            P(),
            P(None, "rows"),
            P(),
        ),
        check_vma=False,
    )
```
